128 devices in a mesh: row: 8 (over x, core), col: 16 (over y, z).
Axes of the slice: x: 4, y: 4, z: 4, core: 2. Of those that a mesh axis runs over, the one named last changes fastest.
Arguments:
- density: float32 [128, 128, 8192], P('row', 'col'), may hold values from -6 to 6
- integrals: bfloat16 [1024, 1024, 1024], P(('row', 'col')), may hold values from -0.046875 to 0.046875
- quartets: int32 [992, 4], replicated, may hold values from 0 to 127
- holder: int32 [992], replicated, may hold values from 0 to 127, as said below
- degeneracy: int32 [992], replicated, may hold values from 1 to 8, as said below
Outputs:
- fock: float32 [128, 128, 8192], P('row', 'col')
The draws below stay inside these ranges and needn't reach their ends.
Inputs may be any that keep to these rules, and one draw needn't show every extreme that they name: `holder`: each device holds at most 8 quartets and some device holds exactly 8; the six blocks (p,q), (r,s), (p,r), (p,s), (q,r), (q,s) of all quartets on one device have pairwise different owners, the owner of block (a, b) being the device at row a // (128 / 8) and col b // (128 / 16). `degeneracy`: powers of two.
All inputs are finite; a program needn't handle non-finite values.
Results may differ from the reference program's by a relative error of at most 0.0029.
Values may be sent and summed in bfloat16 or wider, within the bound.
A program may use at most 256 MiB of HBM per device.

```python
import jax
import jax.numpy as jnp
from jax import lax

BS = 32
PERT = 8
NBLK = 128
QMAX = 8
QUARTETS = 992
N_ROW = 8
N_COL = 16
DEVICES = 128


def shared_draw(key):
    base = jax.random.fold_in(key, 4242)
    key_miss, key_order, key_rows, key_inner, key_degen = jax.random.split(base, 5)
    ratio = N_COL // N_ROW
    groups = N_ROW // 4
    row_span = NBLK // N_ROW
    col_span = NBLK // N_COL
    total_slots = QMAX * DEVICES
    missing = jax.random.permutation(key_miss, DEVICES) < DEVICES // 4
    slot_ids = jnp.arange(total_slots, dtype=jnp.int32)
    slot_dev = (slot_ids // QMAX).astype(jnp.int32)
    slot_pos = (slot_ids % QMAX).astype(jnp.int32)
    dropped = missing[slot_dev] & (slot_pos == QMAX - 1)
    score = dropped.astype(jnp.int32) * total_slots + slot_ids
    kept = jnp.argsort(score)[:QUARTETS]
    holder_ids = slot_dev[kept]
    holder_ids = holder_ids[jax.random.permutation(key_order, QUARTETS)].astype(jnp.int32)
    order = jnp.arange(QUARTETS, dtype=jnp.int32)
    earlier = (holder_ids[None, :] == holder_ids[:, None]) & (order[None, :] < order[:, None])
    rank = jnp.sum(earlier.astype(jnp.int32), axis=1).astype(jnp.int32)
    offset = (rank // (2 * groups)).astype(jnp.int32)
    within = (rank % (2 * groups)).astype(jnp.int32)
    group_id = (within // 2).astype(jnp.int32)
    flipped = (within % 2).astype(jnp.int32)
    perms = jax.vmap(lambda k: jax.random.permutation(k, N_ROW))(jax.random.split(key_rows, DEVICES * ratio)).astype(jnp.int32)
    row_table = perms[holder_ids * ratio + offset]
    picks = (4 * group_id[:, None] + jnp.arange(4, dtype=jnp.int32)[None, :]).astype(jnp.int32)
    chosen_rows = jnp.take_along_axis(row_table, picks, axis=1)
    chosen_rows = jnp.where(flipped[:, None] == 1, chosen_rows[:, ::-1], chosen_rows)
    inner = jax.random.randint(key_inner, (QUARTETS, 4), 0, col_span).astype(jnp.int32)
    inner_first = jax.random.randint(jax.random.fold_in(key_inner, 3), (QUARTETS,), 0, row_span).astype(jnp.int32)
    block_p = chosen_rows[:, 0] * row_span + inner_first
    block_q = (chosen_rows[:, 1] * ratio + offset) * col_span + inner[:, 1]
    block_r = (chosen_rows[:, 2] * ratio + offset) * col_span + inner[:, 2]
    block_s = (chosen_rows[:, 3] * ratio + offset) * col_span + inner[:, 3]
    quartet_ids = jnp.stack([block_p, block_q, block_r, block_s], 1).astype(jnp.int32)
    powers = jax.random.randint(key_degen, (QUARTETS,), 0, 4).astype(jnp.int32)
    degen = jnp.left_shift(jnp.ones_like(powers), powers).astype(jnp.int32)
    return (quartet_ids, holder_ids, degen)


def draw_quartets(key, part):
    return shared_draw(key)[0]


def draw_holder(key, part):
    return shared_draw(key)[1]


def draw_degeneracy(key, part):
    return shared_draw(key)[2]


def steps_of(own_key, dims, cuts, smallest, largest):
    level, own = 1.0, jax.random.fold_in(own_key, 6)
    for axis_at, shards_of in cuts:
        heights = jnp.exp(jax.random.uniform(jax.random.fold_in(own, axis_at), (shards_of,), jnp.float32, smallest / len(cuts), largest / len(cuts)))
        level = level * jnp.repeat(heights, dims[axis_at] // shards_of).reshape([-1 if axis == axis_at else 1 for axis in range(len(dims))])
    return level


def bell_draw(rng, dims, deviation, bound, cuts=(), kind=jnp.bfloat16):
    array = deviation * jax.random.normal(rng, dims, jnp.float32)
    if cuts:
        array = array * steps_of(rng, dims, cuts, -0.22, 0.18)
    return jnp.clip(array, -bound, bound).astype(kind)


def setup_inputs(seed: int = 0) -> dict:
    key_of = jax.random.split(jax.random.key(seed), 6)
    return {
        "density": bell_draw(key_of[0], (NBLK, NBLK, PERT * BS * BS), 1.0, 6.0, ((0, 8), (1, 16)), jnp.float32),
        "integrals": bell_draw(key_of[1], (QMAX * DEVICES, BS * BS, BS * BS), (16 * BS * BS) ** -0.5, 0.046875, ((0, 128),)),
        "quartets": draw_quartets(jax.random.fold_in(key_of[5], 71), 0),
        "holder": draw_holder(jax.random.fold_in(key_of[5], 71), 0),
        "degeneracy": draw_degeneracy(jax.random.fold_in(key_of[5], 71), 0),
    }


HIGH = lax.Precision.HIGHEST


def quartet_terms(block, pair_dens, factor):
    four = block.astype(jnp.float32).reshape(BS, BS, BS, BS)
    d_pq, d_rs, d_pr, d_ps, d_qr, d_qs = [d.astype(jnp.float32) for d in pair_dens]
    j_pq = jnp.einsum("pqrs,krs->kpq", four, d_rs, precision=HIGH)
    j_rs = jnp.einsum("pqrs,kpq->krs", four, d_pq, precision=HIGH)
    k_pr = jnp.einsum("pqrs,kqs->kpr", four, d_qs, precision=HIGH)
    k_ps = jnp.einsum("pqrs,kqr->kps", four, d_qr, precision=HIGH)
    k_qr = jnp.einsum("pqrs,kps->kqr", four, d_ps, precision=HIGH)
    k_qs = jnp.einsum("pqrs,kpr->kqs", four, d_pr, precision=HIGH)
    coul = 2.0 * factor
    exch = -0.5 * factor
    return [coul * j_pq, coul * j_rs, exch * k_pr, exch * k_ps, exch * k_qr, exch * k_qs]


def reference(density, integrals, quartets, holder, degeneracy):
    dens_b = lax.optimization_barrier(density.astype(jnp.bfloat16))
    count = holder.shape[0]
    order = jnp.arange(count, dtype=jnp.int32)
    earlier = (holder[None, :] == holder[:, None]) & (order[None, :] < order[:, None])
    slot_rank = jnp.sum(earlier.astype(jnp.int32), axis=1).astype(jnp.int32)
    slot_of = (holder * QMAX + slot_rank).astype(jnp.int32)
    first_idx = jnp.stack([quartets[:, 0], quartets[:, 2], quartets[:, 0], quartets[:, 0], quartets[:, 1], quartets[:, 1]], 1)
    second_idx = jnp.stack([quartets[:, 1], quartets[:, 3], quartets[:, 2], quartets[:, 3], quartets[:, 2], quartets[:, 3]], 1)
    fock_init = jnp.zeros(density.shape, jnp.float32)

    def one_step(fock_acc, index):
        block = integrals[slot_of[index]]
        rows_six = first_idx[index]
        cols_six = second_idx[index]
        pair_dens = [dens_b[rows_six[t], cols_six[t]].reshape(PERT, BS, BS) for t in range(6)]
        factor = degeneracy[index].astype(jnp.float32)
        terms = quartet_terms(block, pair_dens, factor)
        for t in range(6):
            fock_acc = fock_acc.at[rows_six[t], cols_six[t]].add(terms[t].reshape(-1))
        return fock_acc, None

    fock_out, _ = lax.scan(one_step, fock_init, order)
    return fock_out
```

```python
import functools

import jax
import jax.numpy as jnp
from jax import lax
from jax.experimental import pallas as pl
from jax.experimental.pallas import tpu as pltpu
from jax.sharding import PartitionSpec as P

BS = 32
PERT = 8
SLOTS = 8
N_ROW = 8
N_COL = 16
DEVS = N_ROW * N_COL
ROWS_LOC = 16
COLS_LOC = 8
BLOCKS = ROWS_LOC * COLS_LOC
PITCH = 72
GPITCH = 40
MESH = pl.DeviceIdType.MESH
F32 = jnp.float32
BF16 = jnp.bfloat16
VMEM = pltpu.VMEM
SMEM = pltpu.SMEM


def here():
    return lax.axis_index("row"), lax.axis_index("col")


def enter_all(col_sem):
    r, c = here()
    first = pltpu.get_barrier_semaphore()

    def greet_row(i, _):
        pl.semaphore_signal(first, inc=1, device_id=((r + i) % N_ROW, c), device_id_type=MESH)
        return 0

    def greet_col(i, _):
        pl.semaphore_signal(first, inc=1, device_id=(r, (c + i) % N_COL), device_id_type=MESH)
        return 0

    def pass_on(i, _):
        pl.semaphore_signal(col_sem, inc=1, device_id=(r, (c + i) % N_COL), device_id_type=MESH)
        return 0

    lax.fori_loop(1, N_ROW, greet_row, 0)
    lax.fori_loop(1, N_COL, greet_col, 0)
    pl.semaphore_wait(first, N_ROW + N_COL - 2)
    lax.fori_loop(1, N_COL, pass_on, 0)
    pl.semaphore_wait(col_sem, N_COL - 1)


def partner(step):
    r, c = here()
    return (r + step // N_COL) % N_ROW, (c + step % N_COL) % N_COL


def exchange(src, dst, send_sem, recv_sem):
    r, c = here()
    me = r * N_COL + c

    def post(step, _):
        tr, tc = partner(step)
        pltpu.make_async_remote_copy(
            src_ref=src.at[tr * N_COL + tc],
            dst_ref=dst.at[me],
            send_sem=send_sem,
            recv_sem=recv_sem,
            device_id=(tr, tc),
            device_id_type=MESH,
        ).start()
        return 0

    lax.fori_loop(1, DEVS, post, 0)
    dst[me] = src[me]
    done = pltpu.make_async_remote_copy(
        src_ref=src.at[pl.ds(0, DEVS - 1)],
        dst_ref=dst.at[pl.ds(0, DEVS - 1)],
        send_sem=send_sem,
        recv_sem=recv_sem,
        device_id=(r, c),
        device_id_type=MESH,
    )
    done.wait_send()
    done.wait_recv()


def fetch_kernel(table, dens, out, blocks, send, send_sem, recv_sem, col_sem):
    flat = blocks.reshape(BLOCKS * PITCH, 128)

    def split(a, _):
        for ck in range(64):
            k, c = ck // 8, ck % 8
            flat[pl.ds(a * 8 * PITCH + c * 8 + k, 8, stride=PITCH), :] = dens[a, :, ck * 128 : (ck + 1) * 128]
        return 0

    lax.fori_loop(0, ROWS_LOC, split, 0)

    def pick(h, _):
        send[h] = blocks[table[h]][:64].astype(BF16)
        return 0

    lax.fori_loop(0, DEVS, pick, 0)
    enter_all(col_sem)
    exchange(send, out, send_sem, recv_sem)


def give_kernel(src, out, send_sem, recv_sem, col_sem):
    enter_all(col_sem)
    exchange(src, out, send_sem, recv_sem)


def group_of(shape):
    return lax.broadcasted_iota(jnp.int32, shape, 1) // 32


def nat_fold(parts):
    g = group_of((8, 128))
    lo = g < 2
    ev = g % 2 == 0
    s = []
    for o in parts:
        s.append(jnp.where(g == 0, o[0:8], jnp.where(g == 1, o[8:16], jnp.where(g == 2, o[16:24], o[24:32]))))
    c02 = jnp.where(lo, s[0], s[2]) + pltpu.roll(jnp.where(lo, s[2], s[0]), 64, 1)
    c13 = jnp.where(lo, s[1], s[3]) + pltpu.roll(jnp.where(lo, s[3], s[1]), 64, 1)
    return jnp.where(ev, c02, c13) + jnp.where(ev, pltpu.roll(c02, 96, 1), pltpu.roll(c13, 32, 1))


def spread(d):
    g = group_of((8, 128))
    rolled = [d] + [pltpu.roll(d, 32 * i, 1) for i in range(1, 4)]
    return [
        jnp.concatenate([jnp.where(g == ul, rolled[(ul - xl) % 4], 0.0) for ul in range(4)], 0) for xl in range(4)
    ]


def stacked(src, q, lead, pitch):
    return jnp.concatenate([src[q, pl.ds(lead * pitch, 32), uh * 128 : (uh + 1) * 128] for uh in range(8)], 0)


def cross(tiles, left, d_nat):
    outs, acc = [], None
    for half in range(2):
        exp = spread(d_nat[:, half * 128 : (half + 1) * 128])
        parts = []
        for pair in range(2):
            w = jnp.concatenate([tiles[half * 4 + pair * 2], tiles[half * 4 + pair * 2 + 1]], 1)
            o = jnp.dot(left, w, preferred_element_type=F32)
            parts += [o[:, :128], o[:, 128:]]
            e = jnp.concatenate([exp[pair * 2], exp[pair * 2 + 1]], 1).astype(BF16)
            t = lax.dot_general(e, w, (((1,), (1,)), ((), ())), preferred_element_type=F32)
            acc = t if acc is None else acc + t
        outs.append(nat_fold(parts))
    return outs, acc


def perm_matrix():
    i = lax.broadcasted_iota(jnp.int32, (1024, 1024), 0)
    j = lax.broadcasted_iota(jnp.int32, (1024, 1024), 1)
    return jnp.where((i % 4) * 256 + ((i // 4) % 8) * 32 + i // 32 == j, 1.0, 0.0).astype(BF16)


def rows_of(x):
    return jnp.concatenate([x[:, c * 128 : (c + 1) * 128] for c in range(8)], 0)


def lanes_of(x):
    return jnp.concatenate([x[c * 8 : (c + 1) * 8, :] for c in range(8)], 1)


def quartet_kernel(owners, factor, back, recv, integ, perm, send, a_buf, g_buf, f_buf, d_nat, d_in, d_perm, o_perm, contrib, sem):
    loads = [pltpu.make_async_copy(integ.at[q], a_buf.at[q % 2], sem.at[q % 2]) for q in range(SLOTS)]
    loads[0].start()

    def collect(i, _):
        d_nat[i] = lanes_of(recv[owners[i]].astype(F32))
        return 0

    lax.fori_loop(0, 48, collect, 0)
    for q in range(SLOTS):
        for n, t in enumerate((4, 2)):
            d_in[pl.ds((q * 2 + n) * 8, 8), :] = d_nat[q * 6 + t]
    moved = jnp.dot(d_in[...].astype(BF16), perm[...], preferred_element_type=F32)
    d_perm[...] = moved.reshape(16, 8, 1024)

    def one(q, _):
        slot = q % 2
        pltpu.make_async_copy(integ.at[q], a_buf.at[slot], sem.at[slot]).wait()

        @pl.when(q + 1 < SLOTS)
        def _():
            pltpu.make_async_copy(integ.at[q + 1], a_buf.at[1 - slot], sem.at[1 - slot]).start()

        def widen(x, _):
            for uh in range(8):
                f_buf[uh, pl.ds(x * GPITCH, 32), :] = a_buf[slot, pl.ds(x * 32, 32), uh * 128 : (uh + 1) * 128].astype(F32)
            return 0

        lax.fori_loop(0, 32, widen, 0)

        def regroup(y, _):
            for uh in range(8):
                g_buf[0, pl.ds(y * 32, 32), uh * 128 : (uh + 1) * 128] = f_buf[uh, pl.ds(y, 32, stride=GPITCH), :].astype(BF16)
            return 0

        lax.fori_loop(0, 32, regroup, 0)
        base = q * 6
        fac = factor[q]
        left_ps = jnp.concatenate([d_perm[q * 2][:, u * 256 : (u + 1) * 256] for u in range(4)], 0).astype(BF16)
        left_qs = jnp.concatenate([d_perm[q * 2 + 1][:, u * 256 : (u + 1) * 256] for u in range(4)], 0).astype(BF16)
        d_rs = d_nat[base + 1].astype(BF16)
        j_rs = jnp.zeros((8, 1024), F32)
        k_qr = jnp.zeros((32, 256), F32)
        k_pr = jnp.zeros((32, 256), F32)
        j_pq, k_ps, k_qs = [], [], []
        for xg in range(4):
            cols = slice(xg * 256, (xg + 1) * 256)
            a_rows = a_buf[slot, xg * 256 : (xg + 1) * 256, :]
            j_rs = j_rs + jnp.dot(d_nat[base, :, cols].astype(BF16), a_rows, preferred_element_type=F32)
            j_pq.append(lax.dot_general(d_rs, a_rows, (((1,), (1,)), ((), ())), preferred_element_type=F32))
            tiles = [stacked(a_buf, slot, xg * 8 + i, 32) for i in range(8)]
            outs, acc = cross(tiles, left_ps, d_nat[base + 3, :, cols])
            k_ps += outs
            k_qr = k_qr + acc
            tiles = [stacked(g_buf, 0, xg * 8 + i, 32) for i in range(8)]
            outs, acc = cross(tiles, left_qs, d_nat[base + 5, :, cols])
            k_qs += outs
            k_pr = k_pr + acc
        coul = 2.0 * fac
        exch = -0.5 * fac
        contrib[base] = rows_of(coul * jnp.concatenate(j_pq, 1)).astype(BF16)
        contrib[base + 1] = rows_of(coul * j_rs).astype(BF16)
        contrib[base + 3] = jnp.concatenate([exch * x for x in k_ps], 0).astype(BF16)
        contrib[base + 5] = jnp.concatenate([exch * x for x in k_qs], 0).astype(BF16)
        o_perm[q * 2] = exch * jnp.concatenate([k_qr[u * 8 : (u + 1) * 8] for u in range(4)], 1)
        o_perm[q * 2 + 1] = exch * jnp.concatenate([k_pr[u * 8 : (u + 1) * 8] for u in range(4)], 1)
        return 0

    lax.fori_loop(0, SLOTS, one, 0)
    back_in = o_perm[...].reshape(128, 1024).astype(BF16)
    natural = lax.dot_general(back_in, perm[...], (((1,), (1,)), ((), ())), preferred_element_type=F32)
    for q in range(SLOTS):
        for n, t in enumerate((4, 2)):
            at = (q * 2 + n) * 8
            contrib[q * 6 + t] = rows_of(natural[at : at + 8]).astype(BF16)

    def place(o, _):
        send[o] = contrib[back[o]]
        return 0

    lax.fori_loop(0, DEVS, place, 0)


def scatter_kernel(table, arrived, out, acc):
    def clear(i, _):
        acc[pl.ds(i * PITCH, PITCH), :] = jnp.zeros((PITCH, 128), F32)
        return 0

    lax.fori_loop(0, BLOCKS + 1, clear, 0)

    def add(h, _):
        at = pl.multiple_of(table[h] * PITCH, 8)
        acc[pl.ds(at, 64), :] += arrived[h].astype(F32)
        return 0

    lax.fori_loop(0, DEVS, add, 0)

    def join(a, _):
        for ck in range(64):
            k, c = ck // 8, ck % 8
            out[a, :, ck * 128 : (ck + 1) * 128] = acc[pl.ds(a * 8 * PITCH + c * 8 + k, 8, stride=PITCH), :]
        return 0

    lax.fori_loop(0, ROWS_LOC, join, 0)


def tables(quartets, holder, degeneracy):
    me = lax.axis_index("row") * N_COL + lax.axis_index("col")
    q = quartets.T
    first = jnp.stack([q[0], q[2], q[0], q[0], q[1], q[1]])
    second = jnp.stack([q[1], q[3], q[2], q[3], q[2], q[3]])
    owner = first // ROWS_LOC * N_COL + second // COLS_LOC
    local = first % ROWS_LOC * COLS_LOC + second % COLS_LOC
    asked = jnp.sum(jnp.where(owner == me, local + 1, 0), 0)
    devs = jnp.arange(DEVS, dtype=jnp.int32)
    lid = jnp.sum(jnp.where(holder[None, :] == devs[:, None], asked[None, :], 0), 1)
    pick = jnp.maximum(lid - 1, 0)
    target = jnp.where(lid > 0, lid - 1, BLOCKS)
    own = holder == me
    order = jnp.arange(holder.shape[0], dtype=jnp.int32)
    rank = jnp.sum(jnp.where(own[None, :] & (order[None, :] < order[:, None]), 1, 0), 1)
    sel = own[None, :] & (rank[None, :] == jnp.arange(SLOTS, dtype=jnp.int32)[:, None])
    owners = jnp.sum(jnp.where(sel[:, None, :], owner[None], 0), 2)
    deg = jnp.sum(jnp.where(sel, degeneracy[None, :], 0), 1)
    live = (deg > 0)[:, None]
    flat = jnp.where(live, owners, -1).reshape(-1)
    ids = jnp.arange(48, dtype=jnp.int32)
    back = jnp.sum(jnp.where(flat[None, :] == devs[:, None], ids[None, :], 0), 1)
    return pick, target, owners.reshape(-1), deg.astype(F32), back


def vspec():
    return pl.BlockSpec(memory_space=VMEM)


def sspec():
    return pl.BlockSpec(memory_space=SMEM)


def params(**kw):
    return pltpu.CompilerParams(vmem_limit_bytes=56 * 2**20, **kw)


def local(density, integrals, quartets, holder, degeneracy):
    pick, target, owners, factor, back = tables(quartets, holder, degeneracy)
    wire = jax.ShapeDtypeStruct((DEVS, 64, 128), BF16)
    sems = [pltpu.SemaphoreType.DMA, pltpu.SemaphoreType.DMA, pltpu.SemaphoreType.REGULAR]
    recv = pl.pallas_call(
        fetch_kernel,
        out_shape=wire,
        in_specs=[sspec(), vspec()],
        out_specs=vspec(),
        scratch_shapes=[VMEM((BLOCKS, PITCH, 128), F32), VMEM((DEVS, 64, 128), BF16)] + sems,
        compiler_params=params(collective_id=0, has_side_effects=True),
        name="fetch",
    )(pick, density)
    send = pl.pallas_call(
        quartet_kernel,
        out_shape=wire,
        in_specs=[sspec(), sspec(), sspec(), vspec(), pl.BlockSpec(memory_space=pl.ANY), vspec()],
        out_specs=vspec(),
        scratch_shapes=[
            VMEM((2, 1024, 1024), BF16),
            VMEM((1, 1024, 1024), BF16),
            VMEM((8, 32 * GPITCH, 128), F32),
            VMEM((48, 8, 1024), F32),
            VMEM((128, 1024), F32),
            VMEM((16, 8, 1024), F32),
            VMEM((16, 8, 1024), F32),
            VMEM((48, 64, 128), BF16),
            pltpu.SemaphoreType.DMA((2,)),
        ],
        compiler_params=params(),
        name="quartets",
    )(owners, factor, back, recv, integrals, perm_matrix())
    arrived = pl.pallas_call(
        give_kernel,
        out_shape=wire,
        in_specs=[vspec()],
        out_specs=vspec(),
        scratch_shapes=sems,
        compiler_params=params(collective_id=1, has_side_effects=True),
        name="give",
    )(send)
    return pl.pallas_call(
        scatter_kernel,
        out_shape=jax.ShapeDtypeStruct(density.shape, F32),
        in_specs=[sspec(), vspec()],
        out_specs=vspec(),
        scratch_shapes=[VMEM(((BLOCKS + 1) * PITCH, 128), F32)],
        compiler_params=params(),
        name="scatter",
    )(target, arrived)


def solution(mesh):
    return jax.shard_map(
        local,
        mesh=mesh,
        in_specs=(P("row", "col", None), P(("row", "col"), None, None), P(), P(), P()),
        out_specs=P("row", "col", None),
        check_vma=False,
    )
```

```python
import jax
import jax.numpy as jnp
from jax import lax
from jax.experimental import pallas as pl
from jax.experimental.pallas import tpu as pltpu
from jax.sharding import PartitionSpec as P

BS = 32
PERT = 8
SLOTS = 8
N_ROW = 8
N_COL = 16
DEVS = N_ROW * N_COL
ROWS_LOC = 16
COLS_LOC = 8
BLOCKS = ROWS_LOC * COLS_LOC
PITCH = 72
GPITCH = 40
MESH = pl.DeviceIdType.MESH
F32 = jnp.float32
BF16 = jnp.bfloat16
VMEM = pltpu.VMEM
SMEM = pltpu.SMEM


def here():
    return lax.axis_index("row"), lax.axis_index("col")


def greet():
    r, c = here()
    first = pltpu.get_barrier_semaphore()

    def greet_row(i, _):
        pl.semaphore_signal(first, inc=1, device_id=((r + i) % N_ROW, c), device_id_type=MESH)
        return 0

    def greet_col(i, _):
        pl.semaphore_signal(first, inc=1, device_id=(r, (c + i) % N_COL), device_id_type=MESH)
        return 0

    lax.fori_loop(1, N_ROW, greet_row, 0)
    lax.fori_loop(1, N_COL, greet_col, 0)


def greeted(col_sem):
    r, c = here()

    def pass_on(i, _):
        pl.semaphore_signal(col_sem, inc=1, device_id=(r, (c + i) % N_COL), device_id_type=MESH)
        return 0

    pl.semaphore_wait(pltpu.get_barrier_semaphore(), N_ROW + N_COL - 2)
    lax.fori_loop(1, N_COL, pass_on, 0)


def all_in(col_sem):
    pl.semaphore_wait(col_sem, N_COL - 1)


def partner(step):
    r, c = here()
    return (r + step // N_COL) % N_ROW, (c + step % N_COL) % N_COL


def all_of(src, dst, send_sem, recv_sem):
    return pltpu.make_async_remote_copy(
        src_ref=src.at[pl.ds(0, DEVS - 1)],
        dst_ref=dst.at[pl.ds(0, DEVS - 1)],
        send_sem=send_sem,
        recv_sem=recv_sem,
        device_id=here(),
        device_id_type=MESH,
    )


def post_all(src, dst, send_sem, recv_sem):
    r, c = here()
    me = r * N_COL + c

    def post(step, _):
        tr, tc = partner(step)
        pltpu.make_async_remote_copy(
            src_ref=src.at[tr * N_COL + tc],
            dst_ref=dst.at[me],
            send_sem=send_sem,
            recv_sem=recv_sem,
            device_id=(tr, tc),
            device_id_type=MESH,
        ).start()
        return 0

    lax.fori_loop(1, DEVS, post, 0)
    dst[me] = src[me]


def group_of(shape):
    return lax.broadcasted_iota(jnp.int32, shape, 1) // 32


def nat_fold(parts):
    g = group_of((8, 128))
    lo = g < 2
    ev = g % 2 == 0
    s = []
    for o in parts:
        s.append(jnp.where(g == 0, o[0:8], jnp.where(g == 1, o[8:16], jnp.where(g == 2, o[16:24], o[24:32]))))
    c02 = jnp.where(lo, s[0], s[2]) + pltpu.roll(jnp.where(lo, s[2], s[0]), 64, 1)
    c13 = jnp.where(lo, s[1], s[3]) + pltpu.roll(jnp.where(lo, s[3], s[1]), 64, 1)
    return jnp.where(ev, c02, c13) + jnp.where(ev, pltpu.roll(c02, 96, 1), pltpu.roll(c13, 32, 1))


def spread(d):
    g = group_of((8, 128))
    rolled = [d] + [pltpu.roll(d, 32 * i, 1) for i in range(1, 4)]
    return [
        jnp.concatenate([jnp.where(g == ul, rolled[(ul - xl) % 4], 0.0) for ul in range(4)], 0) for xl in range(4)
    ]


def half_tile(src, q, lead, hf):
    return jnp.concatenate(
        [src[q, pl.ds(pl.multiple_of(lead * 32 + hf * 16, 16), 16), uh * 128 : (uh + 1) * 128] for uh in range(8)], 0
    )


def full_tile(src, q, lead):
    return jnp.concatenate([half_tile(src, q, lead, hf) for hf in range(2)], 0)


def fold_quarter(src, q, left, qt):
    outs = []
    for grp in range(2):
        parts = []
        for pair in range(2):
            lead = qt * 8 + grp * 4 + pair * 2
            w = jnp.concatenate([full_tile(src, q, lead), full_tile(src, q, lead + 1)], 1)
            o = jnp.dot(left, w, preferred_element_type=F32)
            parts += [o[:, :128], o[:, 128:]]
        outs.append(nat_fold(parts))
    return jnp.concatenate(outs, 0)


def spread_half(src, q, d, hf):
    acc = jnp.zeros((32, 128), F32)
    for grp in range(8):
        exp = spread(d[:, grp * 128 : (grp + 1) * 128])
        for pair in range(2):
            lead = grp * 4 + pair * 2
            w = jnp.concatenate([half_tile(src, q, lead, hf), half_tile(src, q, lead + 1, hf)], 1)
            e = jnp.concatenate([exp[pair * 2], exp[pair * 2 + 1]], 1).astype(BF16)
            acc = acc + lax.dot_general(e, w, (((1,), (1,)), ((), ())), preferred_element_type=F32)
    return jnp.concatenate([acc[u * 8 : (u + 1) * 8] for u in range(4)], 1)


def half_perm():
    i = lax.broadcasted_iota(jnp.int32, (512, 512), 0)
    j = lax.broadcasted_iota(jnp.int32, (512, 512), 1)
    return jnp.where((i % 4) * 128 + ((i // 4) % 8) * 16 + i // 32 == j, 1.0, 0.0).astype(BF16)


def two_rows(x):
    return jnp.concatenate([x[:, :128], x[:, 128:]], 0)


def lanes_of(x):
    return jnp.concatenate([x[c * 8 : (c + 1) * 8, :] for c in range(8)], 1)


def fused_kernel(
    pick, owners, factor, back, dens_hbm, integ, out,
    dens, a_all, g_all, work, send, recv, give, d_nat, d_in, left, o_perm, perm, contrib,
    dens_sem, a_sem, send_sem, recv_sem, give_sem, back_sem, col_sem,
):
    r, c = here()
    me = r * N_COL + c
    dens_in = [pltpu.make_async_copy(dens_hbm.at[pl.ds(i * 4, 4)], dens.at[pl.ds(i * 4, 4)], dens_sem.at[i]) for i in range(4)]
    for copy in dens_in:
        copy.start()

    def load(q):
        return pltpu.make_async_copy(integ.at[q], a_all.at[q], a_sem.at[q])

    greet()
    flat = work.reshape(160 * 64, 128)
    for i in range(4):
        dens_in[i].wait()

        def split(a, _):
            for ck in range(64):
                k, cc = ck // 8, ck % 8
                flat[pl.ds(a * 8 * PITCH + cc * 8 + k, 8, stride=PITCH), :] = dens[a, :, ck * 128 : (ck + 1) * 128]
            return 0

        lax.fori_loop(i * 4, i * 4 + 4, split, 0)
    greeted(col_sem)
    for q in range(SLOTS):
        load(q).start()
    blocks = work.at[pl.ds(0, 144)].reshape(BLOCKS, PITCH, 128)

    def choose(h, _):
        send[h] = blocks[pick[h]][:64].astype(BF16)
        return 0

    lax.fori_loop(0, DEVS, choose, 0)
    all_in(col_sem)
    post_all(send, recv, send_sem, recv_sem)
    perm[...] = half_perm()
    wide = work.reshape(8, 32 * GPITCH, 128)

    def regroup(q, _):
        load(q).wait()

        def widen(x, _):
            for uh in range(8):
                wide[uh, pl.ds(x * GPITCH, 32), :] = a_all[q, pl.ds(x * 32, 32), uh * 128 : (uh + 1) * 128].astype(F32)
            return 0

        lax.fori_loop(0, 32, widen, 0)

        def gather(y, _):
            for uh in range(8):
                g_all[q, pl.ds(y * 32, 32), uh * 128 : (uh + 1) * 128] = wide[uh, pl.ds(y, 32, stride=GPITCH), :].astype(BF16)
            return 0

        lax.fori_loop(0, 32, gather, 0)
        return 0

    lax.fori_loop(0, SLOTS, regroup, 0)
    all_of(send, recv, send_sem, recv_sem).wait_recv()

    def collect(i, _):
        d_nat[i] = lanes_of(recv[owners[i]].astype(F32))
        return 0

    lax.fori_loop(0, 48, collect, 0)
    for q in range(SLOTS):
        for n, t in enumerate((4, 2)):
            d_in[pl.ds((q * 2 + n) * 8, 8), :] = d_nat[q * 6 + t]
    for hf in range(2):
        moved = jnp.dot(d_in[:, hf * 512 : (hf + 1) * 512].astype(BF16), perm[...], preferred_element_type=F32)
        for i in range(16):
            rows = moved[i * 8 : (i + 1) * 8]
            left[i, :, hf * 128 : (hf + 1) * 128] = jnp.concatenate(
                [rows[:, u * 128 : (u + 1) * 128] for u in range(4)], 0
            ).astype(BF16)

    def quarter(qt, hf, first):
        span = pl.ds(pl.multiple_of(qt * 256, 256), 256)

        def one(q, _):
            base = q * 6
            coul = 2.0 * factor[q]
            exch = -0.5 * factor[q]
            j_pq = lax.dot_general(
                d_nat[base + 1].astype(BF16), a_all[q, span, :], (((1,), (1,)), ((), ())), preferred_element_type=F32
            )
            contrib[qt, base] = two_rows(coul * j_pq).astype(BF16)
            j_rs = jnp.dot(d_nat[base].astype(BF16), a_all[q, :, span], preferred_element_type=F32)
            contrib[qt, base + 1] = two_rows(coul * j_rs).astype(BF16)
            contrib[qt, base + 3] = (exch * fold_quarter(a_all, q, left[q * 2], qt)).astype(BF16)
            contrib[qt, base + 5] = (exch * fold_quarter(g_all, q, left[q * 2 + 1], qt)).astype(BF16)
            if first:
                o_perm[q * 2] = exch * spread_half(a_all, q, d_nat[base + 3], hf)
                o_perm[q * 2 + 1] = exch * spread_half(g_all, q, d_nat[base + 5], hf)
            return 0

        lax.fori_loop(0, SLOTS, one, 0)
        if first:
            natural = lax.dot_general(
                o_perm[...].reshape(128, 512).astype(BF16), perm[...], (((1,), (1,)), ((), ())), preferred_element_type=F32
            )
            for i in range(16):
                at = (i // 2) * 6 + (4, 2)[i % 2]
                rows = natural[i * 8 : (i + 1) * 8]
                contrib[qt, at] = two_rows(rows[:, :256]).astype(BF16)
                contrib[qt + 1, at] = two_rows(rows[:, 256:]).astype(BF16)

        def place(o, _):
            give[qt, o] = contrib[qt, back[o]]
            return 0

        lax.fori_loop(0, DEVS, place, 0)
        post_all(give.at[qt], out.at[qt], give_sem.at[qt], back_sem.at[qt])

    def half(hf, _):
        quarter(hf * 2, hf, True)
        quarter(hf * 2 + 1, hf, False)
        return 0

    lax.fori_loop(0, 2, half, 0)
    all_of(send, recv, send_sem, recv_sem).wait_send()
    for qt in range(4):
        done = all_of(give.at[qt], out.at[qt], give_sem.at[qt], back_sem.at[qt])
        done.wait_recv()
        done.wait_send()


def scatter_kernel(table, arrived, out, acc):
    def clear(i, _):
        acc[pl.ds(i * PITCH, PITCH), :] = jnp.zeros((PITCH, 128), F32)
        return 0

    lax.fori_loop(0, BLOCKS + 1, clear, 0)

    def add(h, _):
        at = pl.multiple_of(table[h] * PITCH, 8)
        for qt in range(4):
            acc[pl.ds(at + qt * 16, 16), :] += arrived[qt, h].astype(F32)
        return 0

    lax.fori_loop(0, DEVS, add, 0)

    def join(a, _):
        for ck in range(64):
            k, c = ck // 8, ck % 8
            out[a, :, ck * 128 : (ck + 1) * 128] = acc[pl.ds(a * 8 * PITCH + c * 8 + k, 8, stride=PITCH), :]
        return 0

    lax.fori_loop(0, ROWS_LOC, join, 0)


def tables(quartets, holder, degeneracy):
    me = lax.axis_index("row") * N_COL + lax.axis_index("col")
    q = quartets.T
    first = jnp.stack([q[0], q[2], q[0], q[0], q[1], q[1]])
    second = jnp.stack([q[1], q[3], q[2], q[3], q[2], q[3]])
    owner = first // ROWS_LOC * N_COL + second // COLS_LOC
    local = first % ROWS_LOC * COLS_LOC + second % COLS_LOC
    asked = jnp.sum(jnp.where(owner == me, local + 1, 0), 0)
    devs = jnp.arange(DEVS, dtype=jnp.int32)
    lid = jnp.sum(jnp.where(holder[None, :] == devs[:, None], asked[None, :], 0), 1)
    pick = jnp.maximum(lid - 1, 0)
    target = jnp.where(lid > 0, lid - 1, BLOCKS)
    own = holder == me
    order = jnp.arange(holder.shape[0], dtype=jnp.int32)
    rank = jnp.sum(jnp.where(own[None, :] & (order[None, :] < order[:, None]), 1, 0), 1)
    sel = own[None, :] & (rank[None, :] == jnp.arange(SLOTS, dtype=jnp.int32)[:, None])
    owners = jnp.sum(jnp.where(sel[:, None, :], owner[None], 0), 2)
    deg = jnp.sum(jnp.where(sel, degeneracy[None, :], 0), 1)
    live = (deg > 0)[:, None]
    flat = jnp.where(live, owners, -1).reshape(-1)
    ids = jnp.arange(48, dtype=jnp.int32)
    back = jnp.sum(jnp.where(flat[None, :] == devs[:, None], ids[None, :], 0), 1)
    return pick, target, owners.reshape(-1), deg.astype(F32), back


def vspec():
    return pl.BlockSpec(memory_space=VMEM)


def sspec():
    return pl.BlockSpec(memory_space=SMEM)


def params(**kw):
    return pltpu.CompilerParams(vmem_limit_bytes=60 * 2**20, **kw)


def local(density, integrals, quartets, holder, degeneracy):
    pick, target, owners, factor, back = tables(quartets, holder, degeneracy)
    anyspec = pl.BlockSpec(memory_space=pl.ANY)
    dma = pltpu.SemaphoreType.DMA
    arrived = pl.pallas_call(
        fused_kernel,
        out_shape=jax.ShapeDtypeStruct((4, DEVS, 16, 128), BF16),
        in_specs=[sspec(), sspec(), sspec(), sspec(), anyspec, anyspec],
        out_specs=vspec(),
        scratch_shapes=[
            VMEM((ROWS_LOC, COLS_LOC, 8192), F32),
            VMEM((SLOTS, 1024, 1024), BF16),
            VMEM((SLOTS, 1024, 1024), BF16),
            VMEM((160, 64, 128), F32),
            VMEM((DEVS, 64, 128), BF16),
            VMEM((DEVS, 64, 128), BF16),
            VMEM((4, DEVS, 16, 128), BF16),
            VMEM((48, 8, 1024), F32),
            VMEM((128, 1024), F32),
            VMEM((16, 32, 256), BF16),
            VMEM((16, 8, 512), F32),
            VMEM((512, 512), BF16),
            VMEM((4, 48, 16, 128), BF16),
            dma((4,)),
            dma((SLOTS,)),
            dma,
            dma,
            dma((4,)),
            dma((4,)),
            pltpu.SemaphoreType.REGULAR,
        ],
        compiler_params=params(collective_id=0, has_side_effects=True),
        name="fused",
    )(pick, owners, factor, back, density, integrals)
    return pl.pallas_call(
        scatter_kernel,
        out_shape=jax.ShapeDtypeStruct(density.shape, F32),
        in_specs=[sspec(), vspec()],
        out_specs=vspec(),
        scratch_shapes=[VMEM(((BLOCKS + 1) * PITCH, 128), F32)],
        compiler_params=params(),
        name="scatter",
    )(target, arrived)


def solution(mesh):
    return jax.shard_map(
        local,
        mesh=mesh,
        in_specs=(P("row", "col", None), P(("row", "col"), None, None), P(), P(), P()),
        out_specs=P("row", "col", None),
        check_vma=False,
    )
```

```python
import jax
import jax.numpy as jnp
from jax import lax
from jax.experimental import pallas as pl
from jax.experimental.pallas import tpu as pltpu
from jax.sharding import PartitionSpec as P

BS = 32
PERT = 8
SLOTS = 8
N_ROW = 8
N_COL = 16
DEVS = N_ROW * N_COL
ROWS_LOC = 16
COLS_LOC = 8
BLOCKS = ROWS_LOC * COLS_LOC
PITCH = 72
GPITCH = 40
MESH = pl.DeviceIdType.MESH
F32 = jnp.float32
BF16 = jnp.bfloat16
VMEM = pltpu.VMEM
SMEM = pltpu.SMEM


def here():
    return lax.axis_index("row"), lax.axis_index("col")


def greet():
    r, c = here()
    first = pltpu.get_barrier_semaphore()

    def greet_row(i, _):
        pl.semaphore_signal(first, inc=1, device_id=((r + i) % N_ROW, c), device_id_type=MESH)
        return 0

    def greet_col(i, _):
        pl.semaphore_signal(first, inc=1, device_id=(r, (c + i) % N_COL), device_id_type=MESH)
        return 0

    lax.fori_loop(1, N_ROW, greet_row, 0)
    lax.fori_loop(1, N_COL, greet_col, 0)


def greeted(col_sem):
    r, c = here()

    def pass_on(i, _):
        pl.semaphore_signal(col_sem, inc=1, device_id=(r, (c + i) % N_COL), device_id_type=MESH)
        return 0

    pl.semaphore_wait(pltpu.get_barrier_semaphore(), N_ROW + N_COL - 2)
    lax.fori_loop(1, N_COL, pass_on, 0)


def all_in(col_sem):
    pl.semaphore_wait(col_sem, N_COL - 1)


def all_of(src, dst, send_sem, recv_sem):
    return pltpu.make_async_remote_copy(
        src_ref=src.at[pl.ds(0, DEVS - 1)],
        dst_ref=dst.at[pl.ds(0, DEVS - 1)],
        send_sem=send_sem,
        recv_sem=recv_sem,
        device_id=here(),
        device_id_type=MESH,
    )


def post(src, dst, send_sem, recv_sem, tr, tc):
    r, c = here()
    pltpu.make_async_remote_copy(
        src_ref=src.at[tr * N_COL + tc],
        dst_ref=dst.at[r * N_COL + c],
        send_sem=send_sem,
        recv_sem=recv_sem,
        device_id=(tr, tc),
        device_id_type=MESH,
    ).start()


def post_row(src, dst, send_sem, recv_sem, i):
    r, c = here()
    tr = lax.rem(r + i, N_ROW)
    for j in range(1, N_COL):
        post(src, dst, send_sem, recv_sem, tr, lax.rem(c + j, N_COL))

    @pl.when(i < N_ROW - 1)
    def _():
        post(src, dst, send_sem, recv_sem, lax.rem(r + i + 1, N_ROW), c)


def post_all(src, dst, send_sem, recv_sem):
    r, c = here()
    me = r * N_COL + c

    def row(i, _):
        post_row(src, dst, send_sem, recv_sem, i)
        return 0

    lax.fori_loop(0, N_ROW, row, 0)
    dst[me] = src[me]


def group_of(shape):
    return lax.broadcasted_iota(jnp.int32, shape, 1) // 32


def nat_fold(parts):
    g = group_of((8, 128))
    lo = g < 2
    ev = g % 2 == 0
    s = []
    for o in parts:
        s.append(jnp.where(g == 0, o[0:8], jnp.where(g == 1, o[8:16], jnp.where(g == 2, o[16:24], o[24:32]))))
    c02 = jnp.where(lo, s[0], s[2]) + pltpu.roll(jnp.where(lo, s[2], s[0]), 64, 1)
    c13 = jnp.where(lo, s[1], s[3]) + pltpu.roll(jnp.where(lo, s[3], s[1]), 64, 1)
    return jnp.where(ev, c02, c13) + jnp.where(ev, pltpu.roll(c02, 96, 1), pltpu.roll(c13, 32, 1))


def spread(d):
    g = group_of((8, 128))
    rolled = [d] + [pltpu.roll(d, 32 * i, 1) for i in range(1, 4)]
    return [
        jnp.concatenate([jnp.where(g == ul, rolled[(ul - xl) % 4], 0.0) for ul in range(4)], 0) for xl in range(4)
    ]


def half_tile(src, q, lead, hf):
    return jnp.concatenate(
        [src[q, pl.ds(pl.multiple_of(lead * 32 + hf * 16, 16), 16), uh * 128 : (uh + 1) * 128] for uh in range(8)], 0
    )


def fold_quarter(src, q, left, qt, kh):
    outs = []
    for grp in range(2):
        parts = []
        for pair in range(2):
            lead = qt * 8 + grp * 4 + pair * 2
            w = jnp.concatenate([half_tile(src, q, lead, kh), half_tile(src, q, lead + 1, kh)], 1)
            o = jnp.dot(left, w, preferred_element_type=F32)
            parts += [o[:, :128], o[:, 128:]]
        outs.append(nat_fold(parts))
    return jnp.concatenate(outs, 0)


def spread_half(src, q, d, hf, kh):
    acc = jnp.zeros((32, 128), F32)
    for grp in range(4):
        exp = spread(d[:, grp * 128 : (grp + 1) * 128])
        for pair in range(2):
            lead = kh * 16 + grp * 4 + pair * 2
            w = jnp.concatenate([half_tile(src, q, lead, hf), half_tile(src, q, lead + 1, hf)], 1)
            e = jnp.concatenate([exp[pair * 2], exp[pair * 2 + 1]], 1).astype(BF16)
            acc = acc + lax.dot_general(e, w, (((1,), (1,)), ((), ())), preferred_element_type=F32)
    return jnp.concatenate([acc[u * 8 : (u + 1) * 8] for u in range(4)], 1)


def half_perm():
    i = lax.broadcasted_iota(jnp.int32, (512, 512), 0)
    j = lax.broadcasted_iota(jnp.int32, (512, 512), 1)
    return jnp.where((i % 4) * 128 + ((i // 4) % 8) * 16 + i // 32 == j, 1.0, 0.0).astype(BF16)


def two_rows(x):
    return jnp.concatenate([x[:, :128], x[:, 128:]], 0)


def lanes_of(x):
    return jnp.concatenate([x[c * 8 : (c + 1) * 8, :] for c in range(x.shape[0] // 8)], 1)


def fused_kernel(
    pick, owners, factor, back, dens_hbm, integ, out,
    dens, a_all, g_all, work, send, recv0, recv1, give, d_nat, d_in, left, acc, o_acc, o_perm, perm, contrib,
    dens_sem, a_sem, send_sem, recv_sem, give_sem, back_sem, col_sem,
):
    recv = (recv0, recv1)
    dens_in = [pltpu.make_async_copy(dens_hbm.at[pl.ds(i * 4, 4)], dens.at[pl.ds(i * 4, 4)], dens_sem.at[i]) for i in range(4)]
    for copy in dens_in:
        copy.start()

    def load(q):
        return pltpu.make_async_copy(integ.at[q], a_all.at[q], a_sem.at[q])

    greet()
    flat = work.reshape(160 * 64, 128)
    for i in range(4):
        dens_in[i].wait()

        def split(a, _):
            for ck in range(64):
                k, cc = ck // 8, ck % 8
                flat[pl.ds(a * 8 * PITCH + cc * 8 + k, 8, stride=PITCH), :] = dens[a, :, ck * 128 : (ck + 1) * 128]
            return 0

        lax.fori_loop(i * 4, i * 4 + 4, split, 0)
    greeted(col_sem)
    for q in range(SLOTS):
        load(q).start()
    blocks = work.at[pl.ds(0, 144)].reshape(BLOCKS, PITCH, 128)

    def choose(h, _):
        block = blocks[pick[h]].astype(BF16)
        send[0, h] = block[:32]
        send[1, h] = block[32:64]
        return 0

    lax.fori_loop(0, DEVS, choose, 0)
    all_in(col_sem)
    for kh in range(2):
        post_all(send.at[kh], recv[kh], send_sem.at[kh], recv_sem.at[kh])
    perm[...] = half_perm()
    wide = work.reshape(8, 32 * GPITCH, 128)

    def regroup(q, _):
        load(q).wait()

        def widen(x, _):
            for uh in range(8):
                wide[uh, pl.ds(x * GPITCH, 32), :] = a_all[q, pl.ds(x * 32, 32), uh * 128 : (uh + 1) * 128].astype(F32)
            return 0

        lax.fori_loop(0, 32, widen, 0)

        def gather(y, _):
            for uh in range(8):
                g_all[q, pl.ds(y * 32, 32), uh * 128 : (uh + 1) * 128] = wide[uh, pl.ds(y, 32, stride=GPITCH), :].astype(BF16)
            return 0

        lax.fori_loop(0, 32, gather, 0)
        return 0

    lax.fori_loop(0, SLOTS, regroup, 0)
    def take_half(kh):
        all_of(send.at[kh], recv[kh], send_sem.at[kh], recv_sem.at[kh]).wait_recv()

        def collect(q, _):
            for t in range(6):
                d_nat[kh, q * 6 + t] = lanes_of(recv[kh][owners[q * 6 + t]].astype(F32))
            for n, t in enumerate((4, 2)):
                d_in[pl.ds(pl.multiple_of((q * 2 + n) * 8, 8), 8), :] = d_nat[kh, q * 6 + t]
            return 0

        lax.fori_loop(0, SLOTS, collect, 0)
        moved = jnp.dot(d_in[...].astype(BF16), perm[...], preferred_element_type=F32)
        for i in range(16):
            rows = moved[i * 8 : (i + 1) * 8]
            left[kh, i] = jnp.concatenate([rows[:, u * 128 : (u + 1) * 128] for u in range(4)], 0).astype(BF16)

    def coulomb(kh, q, qt):
        span = pl.ds(pl.multiple_of(qt * 256, 256), 256)
        base = q * 6
        j_pq = lax.dot_general(
            d_nat[kh, base + 1].astype(BF16),
            a_all[q, span, kh * 512 : (kh + 1) * 512],
            (((1,), (1,)), ((), ())),
            preferred_element_type=F32,
        )
        j_rs = jnp.dot(
            d_nat[kh, base].astype(BF16), a_all[q, kh * 512 : (kh + 1) * 512, span], preferred_element_type=F32
        )
        return two_rows(j_pq), two_rows(j_rs)

    def first_part(q, _):
        base = q * 6
        for qt in range(4):
            acc[qt, base], acc[qt, base + 1] = coulomb(0, q, qt)
            acc[qt, base + 3] = fold_quarter(a_all, q, left[0, q * 2], qt, 0)
            acc[qt, base + 5] = fold_quarter(g_all, q, left[0, q * 2 + 1], qt, 0)
        for hf in range(2):
            o_acc[hf, q * 2] = spread_half(a_all, q, d_nat[0, base + 3], hf, 0)
            o_acc[hf, q * 2 + 1] = spread_half(g_all, q, d_nat[0, base + 5], hf, 0)
        return 0

    take_half(0)
    lax.fori_loop(0, SLOTS, first_part, 0)
    take_half(1)

    def quarter(qt, hf, first):
        def one(q, _):
            base = q * 6
            coul = 2.0 * factor[q]
            exch = -0.5 * factor[q]
            j_pq, j_rs = coulomb(1, q, qt)
            contrib[qt, base] = (coul * (acc[qt, base] + j_pq)).astype(BF16)
            contrib[qt, base + 1] = (coul * (acc[qt, base + 1] + j_rs)).astype(BF16)
            k_ps = acc[qt, base + 3] + fold_quarter(a_all, q, left[1, q * 2], qt, 1)
            contrib[qt, base + 3] = (exch * k_ps).astype(BF16)
            k_qs = acc[qt, base + 5] + fold_quarter(g_all, q, left[1, q * 2 + 1], qt, 1)
            contrib[qt, base + 5] = (exch * k_qs).astype(BF16)
            if first:
                k_qr = o_acc[hf, q * 2] + spread_half(a_all, q, d_nat[1, base + 3], hf, 1)
                o_perm[q * 2] = exch * k_qr
                k_pr = o_acc[hf, q * 2 + 1] + spread_half(g_all, q, d_nat[1, base + 5], hf, 1)
                o_perm[q * 2 + 1] = exch * k_pr
            return 0

        lax.fori_loop(0, SLOTS, one, 0)
        if first:
            natural = lax.dot_general(
                o_perm[...].reshape(128, 512).astype(BF16), perm[...], (((1,), (1,)), ((), ())), preferred_element_type=F32
            )
            for i in range(16):
                at = (i // 2) * 6 + (4, 2)[i % 2]
                rows = natural[i * 8 : (i + 1) * 8]
                contrib[qt, at] = two_rows(rows[:, :256]).astype(BF16)
                contrib[qt + 1, at] = two_rows(rows[:, 256:]).astype(BF16)

        def place(i, _):
            for j in range(8):
                give[qt, i * 8 + j] = contrib[qt, back[i * 8 + j]]
            return 0

        lax.fori_loop(0, DEVS // 8, place, 0)
        post_all(give.at[qt], out.at[qt], give_sem.at[qt], back_sem.at[qt])

    def half(hf, _):
        quarter(hf * 2, hf, True)
        quarter(hf * 2 + 1, hf, False)
        return 0

    lax.fori_loop(0, 2, half, 0)
    for kh in range(2):
        all_of(send.at[kh], recv[kh], send_sem.at[kh], recv_sem.at[kh]).wait_send()
    for qt in range(4):
        done = all_of(give.at[qt], out.at[qt], give_sem.at[qt], back_sem.at[qt])
        done.wait_recv()
        done.wait_send()


def scatter_kernel(table, arrived, out, acc):
    def clear(i, _):
        acc[pl.ds(i * PITCH, PITCH), :] = jnp.zeros((PITCH, 128), F32)
        return 0

    lax.fori_loop(0, BLOCKS + 1, clear, 0)

    def add(h, _):
        at = pl.multiple_of(table[h] * PITCH, 8)
        for qt in range(4):
            acc[pl.ds(at + qt * 16, 16), :] += arrived[qt, h].astype(F32)
        return 0

    lax.fori_loop(0, DEVS, add, 0)

    def join(a, _):
        for ck in range(64):
            k, c = ck // 8, ck % 8
            out[a, :, ck * 128 : (ck + 1) * 128] = acc[pl.ds(a * 8 * PITCH + c * 8 + k, 8, stride=PITCH), :]
        return 0

    lax.fori_loop(0, ROWS_LOC, join, 0)


def tables(quartets, holder, degeneracy):
    me = lax.axis_index("row") * N_COL + lax.axis_index("col")
    q = quartets.T
    first = jnp.stack([q[0], q[2], q[0], q[0], q[1], q[1]])
    second = jnp.stack([q[1], q[3], q[2], q[3], q[2], q[3]])
    owner = first // ROWS_LOC * N_COL + second // COLS_LOC
    local = first % ROWS_LOC * COLS_LOC + second % COLS_LOC
    asked = jnp.sum(jnp.where(owner == me, local + 1, 0), 0)
    devs = jnp.arange(DEVS, dtype=jnp.int32)
    lid = jnp.sum(jnp.where(holder[None, :] == devs[:, None], asked[None, :], 0), 1)
    pick = jnp.maximum(lid - 1, 0)
    target = jnp.where(lid > 0, lid - 1, BLOCKS)
    own = holder == me
    order = jnp.arange(holder.shape[0], dtype=jnp.int32)
    rank = jnp.sum(jnp.where(own[None, :] & (order[None, :] < order[:, None]), 1, 0), 1)
    sel = own[None, :] & (rank[None, :] == jnp.arange(SLOTS, dtype=jnp.int32)[:, None])
    owners = jnp.sum(jnp.where(sel[:, None, :], owner[None], 0), 2)
    deg = jnp.sum(jnp.where(sel, degeneracy[None, :], 0), 1)
    live = (deg > 0)[:, None]
    flat = jnp.where(live, owners, -1).reshape(-1)
    ids = jnp.arange(48, dtype=jnp.int32)
    back = jnp.sum(jnp.where(flat[None, :] == devs[:, None], ids[None, :], 0), 1)
    return pick, target, owners.reshape(-1), deg.astype(F32), back


def vspec():
    return pl.BlockSpec(memory_space=VMEM)


def sspec():
    return pl.BlockSpec(memory_space=SMEM)


def params(**kw):
    return pltpu.CompilerParams(vmem_limit_bytes=60 * 2**20, **kw)


def local(density, integrals, quartets, holder, degeneracy):
    pick, target, owners, factor, back = tables(quartets, holder, degeneracy)
    anyspec = pl.BlockSpec(memory_space=pl.ANY)
    dma = pltpu.SemaphoreType.DMA
    arrived = pl.pallas_call(
        fused_kernel,
        out_shape=jax.ShapeDtypeStruct((4, DEVS, 16, 128), BF16),
        in_specs=[sspec(), sspec(), sspec(), sspec(), anyspec, anyspec],
        out_specs=vspec(),
        scratch_shapes=[
            VMEM((ROWS_LOC, COLS_LOC, 8192), F32),
            VMEM((SLOTS, 1024, 1024), BF16),
            VMEM((SLOTS, 1024, 1024), BF16),
            VMEM((160, 64, 128), F32),
            VMEM((2, DEVS, 32, 128), BF16),
            VMEM((DEVS, 32, 128), BF16),
            VMEM((DEVS, 32, 128), BF16),
            VMEM((4, DEVS, 16, 128), BF16),
            VMEM((2, 48, 8, 512), F32),
            VMEM((128, 512), F32),
            VMEM((2, 16, 32, 128), BF16),
            VMEM((4, 48, 16, 128), F32),
            VMEM((2, 16, 8, 512), F32),
            VMEM((16, 8, 512), F32),
            VMEM((512, 512), BF16),
            VMEM((4, 48, 16, 128), BF16),
            dma((4,)),
            dma((SLOTS,)),
            dma((2,)),
            dma((2,)),
            dma((4,)),
            dma((4,)),
            pltpu.SemaphoreType.REGULAR,
        ],
        compiler_params=params(collective_id=0, has_side_effects=True),
        name="fused",
    )(pick, owners, factor, back, density, integrals)
    return pl.pallas_call(
        scatter_kernel,
        out_shape=jax.ShapeDtypeStruct(density.shape, F32),
        in_specs=[sspec(), vspec()],
        out_specs=vspec(),
        scratch_shapes=[VMEM(((BLOCKS + 1) * PITCH, 128), F32)],
        compiler_params=params(),
        name="scatter",
    )(target, arrived)


def solution(mesh):
    return jax.shard_map(
        local,
        mesh=mesh,
        in_specs=(P("row", "col", None), P(("row", "col"), None, None), P(), P(), P()),
        out_specs=P("row", "col", None),
        check_vma=False,
    )
```

```python
import jax
import jax.numpy as jnp
from jax import lax
from jax.experimental import pallas as pl
from jax.experimental.pallas import tpu as pltpu
from jax.sharding import PartitionSpec as P

BS = 32
PERT = 8
SLOTS = 8
N_ROW = 8
N_COL = 16
DEVS = N_ROW * N_COL
ROWS_LOC = 16
COLS_LOC = 8
BLOCKS = ROWS_LOC * COLS_LOC
PITCH = 72
GPITCH = 40
MESH = pl.DeviceIdType.MESH
F32 = jnp.float32
BF16 = jnp.bfloat16
VMEM = pltpu.VMEM
SMEM = pltpu.SMEM


def here():
    return lax.axis_index("row"), lax.axis_index("col")


def greet():
    r, c = here()
    first = pltpu.get_barrier_semaphore()

    def greet_row(i, _):
        pl.semaphore_signal(first, inc=1, device_id=((r + i) % N_ROW, c), device_id_type=MESH)
        return 0

    def greet_col(i, _):
        pl.semaphore_signal(first, inc=1, device_id=(r, (c + i) % N_COL), device_id_type=MESH)
        return 0

    lax.fori_loop(1, N_ROW, greet_row, 0)
    lax.fori_loop(1, N_COL, greet_col, 0)


def greeted(col_sem):
    r, c = here()

    def pass_on(i, _):
        pl.semaphore_signal(col_sem, inc=1, device_id=(r, (c + i) % N_COL), device_id_type=MESH)
        return 0

    pl.semaphore_wait(pltpu.get_barrier_semaphore(), N_ROW + N_COL - 2)
    lax.fori_loop(1, N_COL, pass_on, 0)


def all_in(col_sem):
    pl.semaphore_wait(col_sem, N_COL - 1)


def all_of(src, dst, send_sem, recv_sem):
    return pltpu.make_async_remote_copy(
        src_ref=src.at[pl.ds(0, DEVS - 1)],
        dst_ref=dst.at[pl.ds(0, DEVS - 1)],
        send_sem=send_sem,
        recv_sem=recv_sem,
        device_id=here(),
        device_id_type=MESH,
    )


def post(src, dst, send_sem, recv_sem, tr, tc):
    r, c = here()
    pltpu.make_async_remote_copy(
        src_ref=src.at[tr * N_COL + tc],
        dst_ref=dst.at[r * N_COL + c],
        send_sem=send_sem,
        recv_sem=recv_sem,
        device_id=(tr, tc),
        device_id_type=MESH,
    ).start()


def post_row(src, dst, send_sem, recv_sem, i):
    r, c = here()
    tr = lax.rem(r + i, N_ROW)
    for j in range(1, N_COL):
        post(src, dst, send_sem, recv_sem, tr, lax.rem(c + j, N_COL))

    @pl.when(i < N_ROW - 1)
    def _():
        post(src, dst, send_sem, recv_sem, lax.rem(r + i + 1, N_ROW), c)


def post_all(src, dst, send_sem, recv_sem):
    r, c = here()
    me = r * N_COL + c

    def row(i, _):
        post_row(src, dst, send_sem, recv_sem, i)
        return 0

    lax.fori_loop(0, N_ROW, row, 0)
    dst[me] = src[me]


def group_of(shape):
    return lax.broadcasted_iota(jnp.int32, shape, 1) // 32


def nat_fold(parts):
    g = group_of((8, 128))
    lo = g < 2
    ev = g % 2 == 0
    s = []
    for o in parts:
        s.append(jnp.where(g == 0, o[0:8], jnp.where(g == 1, o[8:16], jnp.where(g == 2, o[16:24], o[24:32]))))
    c02 = jnp.where(lo, s[0], s[2]) + pltpu.roll(jnp.where(lo, s[2], s[0]), 64, 1)
    c13 = jnp.where(lo, s[1], s[3]) + pltpu.roll(jnp.where(lo, s[3], s[1]), 64, 1)
    return jnp.where(ev, c02, c13) + jnp.where(ev, pltpu.roll(c02, 96, 1), pltpu.roll(c13, 32, 1))


def spread(d):
    g = group_of((8, 128))
    rolled = [d] + [pltpu.roll(d, 32 * i, 1) for i in range(1, 4)]
    return [
        jnp.concatenate([jnp.where(g == ul, rolled[(ul - xl) % 4], 0.0) for ul in range(4)], 0) for xl in range(4)
    ]


def half_tile(src, q, lead, hf):
    return jnp.concatenate(
        [src[q, pl.ds(pl.multiple_of(lead * 32 + hf * 16, 16), 16), uh * 128 : (uh + 1) * 128] for uh in range(8)], 0
    )


def fold_quarter(src, q, left, qt, kh):
    outs = []
    for grp in range(2):
        parts = []
        for pair in range(2):
            lead = qt * 8 + grp * 4 + pair * 2
            w = jnp.concatenate([half_tile(src, q, lead, kh), half_tile(src, q, lead + 1, kh)], 1)
            o = jnp.dot(left, w, preferred_element_type=F32)
            parts += [o[:, :128], o[:, 128:]]
        outs.append(nat_fold(parts))
    return jnp.concatenate(outs, 0)


def spread_half(src, q, d, hf, kh):
    acc = jnp.zeros((32, 128), F32)
    for grp in range(4):
        exp = spread(d[:, grp * 128 : (grp + 1) * 128])
        for pair in range(2):
            lead = kh * 16 + grp * 4 + pair * 2
            w = jnp.concatenate([half_tile(src, q, lead, hf), half_tile(src, q, lead + 1, hf)], 1)
            e = jnp.concatenate([exp[pair * 2], exp[pair * 2 + 1]], 1).astype(BF16)
            acc = acc + lax.dot_general(e, w, (((1,), (1,)), ((), ())), preferred_element_type=F32)
    return jnp.concatenate([acc[u * 8 : (u + 1) * 8] for u in range(4)], 1)


def half_perm():
    i = lax.broadcasted_iota(jnp.int32, (512, 512), 0)
    j = lax.broadcasted_iota(jnp.int32, (512, 512), 1)
    return jnp.where((i % 4) * 128 + ((i // 4) % 8) * 16 + i // 32 == j, 1.0, 0.0).astype(BF16)


def two_rows(x):
    return jnp.concatenate([x[:, :128], x[:, 128:]], 0)


def lanes_of(x):
    return jnp.concatenate([x[c * 8 : (c + 1) * 8, :] for c in range(x.shape[0] // 8)], 1)


def make_tables(data, tabs, facs):
    r, c = here()
    me = r * N_COL + c
    first = [data[i : i + 1, :] for i in (0, 2, 0, 0, 1, 1)]
    second = [data[i : i + 1, :] for i in (1, 3, 2, 3, 2, 3)]
    holder = data[4:5, :]
    owner = [f // ROWS_LOC * N_COL + s // COLS_LOC for f, s in zip(first, second)]
    asked = jnp.zeros((1, 1024), jnp.int32)
    for o, f, s in zip(owner, first, second):
        asked += jnp.where((o == me) & (holder >= 0), f % ROWS_LOC * COLS_LOC + s % COLS_LOC + 1, 0)
    dev = lax.broadcasted_iota(jnp.int32, (DEVS, 1024), 0)
    hot = jnp.where(dev == holder, 1.0, 0.0).astype(BF16)
    wanted = jnp.broadcast_to(asked.astype(F32), (8, 1024)).astype(BF16)
    lid = lax.dot_general(wanted, hot, (((1,), (1,)), ((), ())), preferred_element_type=F32)[0:1].astype(jnp.int32)
    own = jnp.broadcast_to(jnp.where(holder == me, 1, 0), (8, 1024))
    lane = lax.broadcasted_iota(jnp.int32, (8, 1024), 1)
    count = own
    for shift in (1, 2, 4, 8, 16, 32, 64, 128, 256, 512):
        count = count + jnp.where(lane >= shift, pltpu.roll(count, shift, 1), 0)
    slot = lax.broadcasted_iota(jnp.int32, (8, 1024), 0)
    sel = (own > 0) & (count - 1 == slot)
    deg = jnp.sum(jnp.where(sel, data[5:6, :].astype(F32), 0.0), 1, keepdims=True)
    col = lax.broadcasted_iota(jnp.int32, (8, DEVS), 1)
    row = lax.broadcasted_iota(jnp.int32, (8, DEVS), 0)
    owners = jnp.zeros((8, DEVS), F32)
    back = jnp.zeros((8, DEVS), F32)
    for t in range(6):
        of = jnp.sum(jnp.where(sel, owner[t].astype(F32), 0.0), 1, keepdims=True)
        owners = jnp.where(col == t, of, owners)
        back += jnp.where((of == col.astype(F32)) & (deg > 0.0), (row * 6 + t).astype(F32), 0.0)
    back = jnp.sum(back, 0, keepdims=True).astype(jnp.int32)
    tabs[3:8, :] = jnp.zeros((5, DEVS), jnp.int32)
    lid = jnp.clip(lid, 0, BLOCKS)
    tabs[0:1, :] = jnp.maximum(lid - 1, 0)
    tabs[1:2, :] = jnp.where(lid > 0, lid - 1, BLOCKS)
    tabs[2:3, :] = jnp.clip(back, 0, 6 * SLOTS - 1)
    tabs[8:16, :] = jnp.clip(owners.astype(jnp.int32), 0, DEVS - 1)
    facs[...] = jnp.broadcast_to(deg, (8, DEVS))


def fused_kernel(
    data, dens_hbm, integ, out, tabs_out,
    tabs_v, facs_v, tabs, facs, tab_sem,
    dens, a_all, g_all, work, send, recv0, recv1, give, d_nat, d_in, left, acc, o_acc, o_perm, perm, contrib,
    dens_sem, a_sem, send_sem, recv_sem, give_sem, back_sem, col_sem,
):
    recv = (recv0, recv1)
    dens_in = [pltpu.make_async_copy(dens_hbm.at[pl.ds(i * 4, 4)], dens.at[pl.ds(i * 4, 4)], dens_sem.at[i]) for i in range(4)]
    for copy in dens_in:
        copy.start()

    def load(q):
        return pltpu.make_async_copy(integ.at[q], a_all.at[q], a_sem.at[q])

    greet()
    make_tables(data, tabs_v, facs_v)
    tab_in = [pltpu.make_async_copy(tabs_v, tabs, tab_sem.at[0]), pltpu.make_async_copy(facs_v, facs, tab_sem.at[1])]
    for copy in tab_in:
        copy.start()
    flat = work.reshape(160 * 64, 128)
    for i in range(4):
        dens_in[i].wait()

        def split(a, _):
            for ck in range(64):
                k, cc = ck // 8, ck % 8
                flat[pl.ds(a * 8 * PITCH + cc * 8 + k, 8, stride=PITCH), :] = dens[a, :, ck * 128 : (ck + 1) * 128]
            return 0

        lax.fori_loop(i * 4, i * 4 + 4, split, 0)
    greeted(col_sem)
    for q in range(SLOTS):
        load(q).start()
    blocks = work.at[pl.ds(0, 144)].reshape(BLOCKS, PITCH, 128)

    for copy in tab_in:
        copy.wait()
    tabs_out[...] = tabs_v[...]

    def choose(h, _):
        block = blocks[tabs[0, h]].astype(BF16)
        send[0, h] = block[:32]
        send[1, h] = block[32:64]
        return 0

    lax.fori_loop(0, DEVS, choose, 0)
    all_in(col_sem)
    for kh in range(2):
        post_all(send.at[kh], recv[kh], send_sem.at[kh], recv_sem.at[kh])
    perm[...] = half_perm()
    wide = work.reshape(8, 32 * GPITCH, 128)

    def regroup(q, _):
        load(q).wait()

        def widen(x, _):
            for uh in range(8):
                wide[uh, pl.ds(x * GPITCH, 32), :] = a_all[q, pl.ds(x * 32, 32), uh * 128 : (uh + 1) * 128].astype(F32)
            return 0

        lax.fori_loop(0, 32, widen, 0)

        def gather(y, _):
            for uh in range(8):
                g_all[q, pl.ds(y * 32, 32), uh * 128 : (uh + 1) * 128] = wide[uh, pl.ds(y, 32, stride=GPITCH), :].astype(BF16)
            return 0

        lax.fori_loop(0, 32, gather, 0)
        return 0

    lax.fori_loop(0, SLOTS, regroup, 0)
    def take_half(kh):
        all_of(send.at[kh], recv[kh], send_sem.at[kh], recv_sem.at[kh]).wait_recv()

        def collect(q, _):
            for t in range(6):
                d_nat[kh, q * 6 + t] = lanes_of(recv[kh][tabs[8 + q, t]].astype(F32))
            for n, t in enumerate((4, 2)):
                d_in[pl.ds(pl.multiple_of((q * 2 + n) * 8, 8), 8), :] = d_nat[kh, q * 6 + t]
            return 0

        lax.fori_loop(0, SLOTS, collect, 0)
        moved = jnp.dot(d_in[...].astype(BF16), perm[...], preferred_element_type=F32)
        for i in range(16):
            rows = moved[i * 8 : (i + 1) * 8]
            left[kh, i] = jnp.concatenate([rows[:, u * 128 : (u + 1) * 128] for u in range(4)], 0).astype(BF16)

    def coulomb(kh, q, qt):
        span = pl.ds(pl.multiple_of(qt * 256, 256), 256)
        base = q * 6
        j_pq = lax.dot_general(
            d_nat[kh, base + 1].astype(BF16),
            a_all[q, span, kh * 512 : (kh + 1) * 512],
            (((1,), (1,)), ((), ())),
            preferred_element_type=F32,
        )
        j_rs = jnp.dot(
            d_nat[kh, base].astype(BF16), a_all[q, kh * 512 : (kh + 1) * 512, span], preferred_element_type=F32
        )
        return two_rows(j_pq), two_rows(j_rs)

    def first_part(q, _):
        base = q * 6
        for qt in range(4):
            acc[qt, base], acc[qt, base + 1] = coulomb(0, q, qt)
            acc[qt, base + 3] = fold_quarter(a_all, q, left[0, q * 2], qt, 0)
            acc[qt, base + 5] = fold_quarter(g_all, q, left[0, q * 2 + 1], qt, 0)
        for hf in range(2):
            o_acc[hf, q * 2] = spread_half(a_all, q, d_nat[0, base + 3], hf, 0)
            o_acc[hf, q * 2 + 1] = spread_half(g_all, q, d_nat[0, base + 5], hf, 0)
        return 0

    take_half(0)
    lax.fori_loop(0, SLOTS, first_part, 0)
    take_half(1)

    def quarter(qt, hf, first):
        def one(q, _):
            base = q * 6
            coul = 2.0 * facs[q, 0]
            exch = -0.5 * facs[q, 0]
            j_pq, j_rs = coulomb(1, q, qt)
            contrib[qt, base] = (coul * (acc[qt, base] + j_pq)).astype(BF16)
            contrib[qt, base + 1] = (coul * (acc[qt, base + 1] + j_rs)).astype(BF16)
            k_ps = acc[qt, base + 3] + fold_quarter(a_all, q, left[1, q * 2], qt, 1)
            contrib[qt, base + 3] = (exch * k_ps).astype(BF16)
            k_qs = acc[qt, base + 5] + fold_quarter(g_all, q, left[1, q * 2 + 1], qt, 1)
            contrib[qt, base + 5] = (exch * k_qs).astype(BF16)
            if first:
                k_qr = o_acc[hf, q * 2] + spread_half(a_all, q, d_nat[1, base + 3], hf, 1)
                o_perm[q * 2] = exch * k_qr
                k_pr = o_acc[hf, q * 2 + 1] + spread_half(g_all, q, d_nat[1, base + 5], hf, 1)
                o_perm[q * 2 + 1] = exch * k_pr
            return 0

        lax.fori_loop(0, SLOTS, one, 0)
        if first:
            natural = lax.dot_general(
                o_perm[...].reshape(128, 512).astype(BF16), perm[...], (((1,), (1,)), ((), ())), preferred_element_type=F32
            )
            for i in range(16):
                at = (i // 2) * 6 + (4, 2)[i % 2]
                rows = natural[i * 8 : (i + 1) * 8]
                contrib[qt, at] = two_rows(rows[:, :256]).astype(BF16)
                contrib[qt + 1, at] = two_rows(rows[:, 256:]).astype(BF16)

        def place(i, _):
            for j in range(8):
                give[qt, i * 8 + j] = contrib[qt, tabs[2, i * 8 + j]]
            return 0

        lax.fori_loop(0, DEVS // 8, place, 0)
        post_all(give.at[qt], out.at[qt], give_sem.at[qt], back_sem.at[qt])

    def half(hf, _):
        quarter(hf * 2, hf, True)
        quarter(hf * 2 + 1, hf, False)
        return 0

    lax.fori_loop(0, 2, half, 0)
    for kh in range(2):
        all_of(send.at[kh], recv[kh], send_sem.at[kh], recv_sem.at[kh]).wait_send()
    for qt in range(4):
        done = all_of(give.at[qt], out.at[qt], give_sem.at[qt], back_sem.at[qt])
        done.wait_recv()
        done.wait_send()


def scatter_kernel(tabs, arrived, out, land, acc, whole, in_sem, out_sem):
    loads = [pltpu.make_async_copy(arrived.at[qt], land.at[qt], in_sem.at[qt]) for qt in range(4)]
    stores = [pltpu.make_async_copy(whole.at[pl.ds(i * 4, 4)], out.at[pl.ds(i * 4, 4)], out_sem.at[i]) for i in range(4)]
    for copy in loads:
        copy.start()

    def clear(i, _):
        acc[pl.ds(i * PITCH, PITCH), :] = jnp.zeros((PITCH, 128), F32)
        return 0

    lax.fori_loop(0, BLOCKS, clear, 0, unroll=4)
    for copy in loads:
        copy.wait()

    def add(h, _):
        at = pl.multiple_of(tabs[1, h] * PITCH, 8)
        more = jnp.concatenate([land[qt, h].astype(F32) for qt in range(4)], 0)
        acc[pl.ds(at, 64), :] += more
        return 0

    lax.fori_loop(0, DEVS, add, 0, unroll=4)
    for i in range(4):

        def join(a, _):
            for ck in range(64):
                k, c = ck // 8, ck % 8
                whole[a, :, ck * 128 : (ck + 1) * 128] = acc[pl.ds(a * 8 * PITCH + c * 8 + k, 8, stride=PITCH), :]
            return 0

        lax.fori_loop(i * 4, i * 4 + 4, join, 0)
        stores[i].start()
    for copy in stores:
        copy.wait()


def vspec():
    return pl.BlockSpec(memory_space=VMEM)


def sspec():
    return pl.BlockSpec(memory_space=SMEM)


def params(**kw):
    return pltpu.CompilerParams(vmem_limit_bytes=60 * 2**20, **kw)


def local(density, integrals, quartets, holder, degeneracy):
    data = jnp.concatenate([quartets.T, holder[None], degeneracy[None]], 0)
    data = jnp.pad(data, ((0, 2), (0, 1024 - data.shape[1])), constant_values=-1)
    anyspec = pl.BlockSpec(memory_space=pl.ANY)
    dma = pltpu.SemaphoreType.DMA
    arrived, tabs = pl.pallas_call(
        fused_kernel,
        out_shape=[jax.ShapeDtypeStruct((4, DEVS, 16, 128), BF16), jax.ShapeDtypeStruct((16, DEVS), jnp.int32)],
        in_specs=[vspec(), anyspec, anyspec],
        out_specs=[vspec(), vspec()],
        scratch_shapes=[
            VMEM((16, DEVS), jnp.int32),
            VMEM((8, DEVS), F32),
            SMEM((16, DEVS), jnp.int32),
            SMEM((8, DEVS), F32),
            dma((2,)),
            VMEM((ROWS_LOC, COLS_LOC, 8192), F32),
            VMEM((SLOTS, 1024, 1024), BF16),
            VMEM((SLOTS, 1024, 1024), BF16),
            VMEM((160, 64, 128), F32),
            VMEM((2, DEVS, 32, 128), BF16),
            VMEM((DEVS, 32, 128), BF16),
            VMEM((DEVS, 32, 128), BF16),
            VMEM((4, DEVS, 16, 128), BF16),
            VMEM((2, 48, 8, 512), F32),
            VMEM((128, 512), F32),
            VMEM((2, 16, 32, 128), BF16),
            VMEM((4, 48, 16, 128), F32),
            VMEM((2, 16, 8, 512), F32),
            VMEM((16, 8, 512), F32),
            VMEM((512, 512), BF16),
            VMEM((4, 48, 16, 128), BF16),
            dma((4,)),
            dma((SLOTS,)),
            dma((2,)),
            dma((2,)),
            dma((4,)),
            dma((4,)),
            pltpu.SemaphoreType.REGULAR,
        ],
        compiler_params=params(collective_id=0, has_side_effects=True),
        name="fused",
    )(data, density, integrals)
    return pl.pallas_call(
        scatter_kernel,
        out_shape=jax.ShapeDtypeStruct(density.shape, F32),
        in_specs=[sspec(), anyspec],
        out_specs=anyspec,
        scratch_shapes=[
            VMEM((4, DEVS, 16, 128), BF16),
            VMEM(((BLOCKS + 1) * PITCH, 128), F32),
            VMEM(density.shape, F32),
            dma((4,)),
            dma((4,)),
        ],
        compiler_params=params(),
        name="scatter",
    )(tabs, arrived)


def solution(mesh):
    return jax.shard_map(
        local,
        mesh=mesh,
        in_specs=(P("row", "col", None), P(("row", "col"), None, None), P(), P(), P()),
        out_specs=P("row", "col", None),
        check_vma=False,
    )
```

```python
import jax
import jax.numpy as jnp
from jax import lax
from jax.experimental import pallas as pl
from jax.experimental.pallas import tpu as pltpu
from jax.sharding import PartitionSpec as P

BS = 32
PERT = 8
SLOTS = 8
N_ROW = 8
N_COL = 16
DEVS = N_ROW * N_COL
ROWS_LOC = 16
COLS_LOC = 8
BLOCKS = ROWS_LOC * COLS_LOC
PITCH = 72
GPITCH = 40
MESH = pl.DeviceIdType.MESH
F32 = jnp.float32
BF16 = jnp.bfloat16
VMEM = pltpu.VMEM
SMEM = pltpu.SMEM


def here():
    return lax.axis_index("row"), lax.axis_index("col")


def greet():
    r, c = here()
    first = pltpu.get_barrier_semaphore()

    def greet_row(i, _):
        pl.semaphore_signal(first, inc=1, device_id=((r + i) % N_ROW, c), device_id_type=MESH)
        return 0

    def greet_col(i, _):
        pl.semaphore_signal(first, inc=1, device_id=(r, (c + i) % N_COL), device_id_type=MESH)
        return 0

    lax.fori_loop(1, N_ROW, greet_row, 0)
    lax.fori_loop(1, N_COL, greet_col, 0)


def greeted(col_sem):
    r, c = here()

    def pass_on(i, _):
        pl.semaphore_signal(col_sem, inc=1, device_id=(r, (c + i) % N_COL), device_id_type=MESH)
        return 0

    pl.semaphore_wait(pltpu.get_barrier_semaphore(), N_ROW + N_COL - 2)
    lax.fori_loop(1, N_COL, pass_on, 0)


def all_in(col_sem):
    pl.semaphore_wait(col_sem, N_COL - 1)


def all_of(src, dst, send_sem, recv_sem):
    return pltpu.make_async_remote_copy(
        src_ref=src.at[pl.ds(0, DEVS - 1)],
        dst_ref=dst.at[pl.ds(0, DEVS - 1)],
        send_sem=send_sem,
        recv_sem=recv_sem,
        device_id=here(),
        device_id_type=MESH,
    )


def post(src, dst, send_sem, recv_sem, tr, tc):
    r, c = here()
    pltpu.make_async_remote_copy(
        src_ref=src.at[tr * N_COL + tc],
        dst_ref=dst.at[r * N_COL + c],
        send_sem=send_sem,
        recv_sem=recv_sem,
        device_id=(tr, tc),
        device_id_type=MESH,
    ).start()


def post_row(src, dst, send_sem, recv_sem, i):
    r, c = here()
    tr = lax.rem(r + i, N_ROW)
    for j in range(1, N_COL):
        post(src, dst, send_sem, recv_sem, tr, lax.rem(c + j, N_COL))

    @pl.when(i < N_ROW - 1)
    def _():
        post(src, dst, send_sem, recv_sem, lax.rem(r + i + 1, N_ROW), c)


def post_all(src, dst, send_sem, recv_sem):
    r, c = here()
    me = r * N_COL + c

    def row(i, _):
        post_row(src, dst, send_sem, recv_sem, i)
        return 0

    lax.fori_loop(0, N_ROW, row, 0)
    dst[me] = src[me]


def group_of(shape):
    return lax.broadcasted_iota(jnp.int32, shape, 1) // 32


def nat_fold(parts):
    g = group_of((8, 128))
    lo = g < 2
    ev = g % 2 == 0
    s = []
    for o in parts:
        s.append(jnp.where(g == 0, o[0:8], jnp.where(g == 1, o[8:16], jnp.where(g == 2, o[16:24], o[24:32]))))
    c02 = jnp.where(lo, s[0], s[2]) + pltpu.roll(jnp.where(lo, s[2], s[0]), 64, 1)
    c13 = jnp.where(lo, s[1], s[3]) + pltpu.roll(jnp.where(lo, s[3], s[1]), 64, 1)
    return jnp.where(ev, c02, c13) + jnp.where(ev, pltpu.roll(c02, 96, 1), pltpu.roll(c13, 32, 1))


def spread(d):
    g = group_of((8, 128))
    rolled = [d] + [pltpu.roll(d, 32 * i, 1) for i in range(1, 4)]
    return [
        jnp.concatenate([jnp.where(g == ul, rolled[(ul - xl) % 4], 0.0) for ul in range(4)], 0) for xl in range(4)
    ]


def half_tile(src, q, lead, hf):
    return jnp.concatenate(
        [src[q, pl.ds(pl.multiple_of(lead * 32 + hf * 16, 16), 16), uh * 128 : (uh + 1) * 128] for uh in range(8)], 0
    )


def fold_quarter(src, q, left, qt, kh):
    outs = []
    for grp in range(2):
        parts = []
        for pair in range(2):
            lead = qt * 8 + grp * 4 + pair * 2
            w = jnp.concatenate([half_tile(src, q, lead, kh), half_tile(src, q, lead + 1, kh)], 1)
            o = jnp.dot(left, w, preferred_element_type=F32)
            parts += [o[:, :128], o[:, 128:]]
        outs.append(nat_fold(parts))
    return jnp.concatenate(outs, 0)


def spread_half(src, q, d, hf, kh):
    acc = jnp.zeros((32, 128), F32)
    for grp in range(4):
        exp = spread(d[:, grp * 128 : (grp + 1) * 128])
        for pair in range(2):
            lead = kh * 16 + grp * 4 + pair * 2
            w = jnp.concatenate([half_tile(src, q, lead, hf), half_tile(src, q, lead + 1, hf)], 1)
            e = jnp.concatenate([exp[pair * 2], exp[pair * 2 + 1]], 1).astype(BF16)
            acc = acc + lax.dot_general(e, w, (((1,), (1,)), ((), ())), preferred_element_type=F32)
    return jnp.concatenate([acc[u * 8 : (u + 1) * 8] for u in range(4)], 1)


def half_perm():
    i = lax.broadcasted_iota(jnp.int32, (512, 512), 0)
    j = lax.broadcasted_iota(jnp.int32, (512, 512), 1)
    return jnp.where((i % 4) * 128 + ((i // 4) % 8) * 16 + i // 32 == j, 1.0, 0.0).astype(BF16)


def two_rows(x):
    return jnp.concatenate([x[:, :128], x[:, 128:]], 0)


def lanes_of(x):
    return jnp.concatenate([x[c * 8 : (c + 1) * 8, :] for c in range(x.shape[0] // 8)], 1)


def make_tables(data, tabs, facs):
    r, c = here()
    me = r * N_COL + c
    first = [data[i : i + 1, :] for i in (0, 2, 0, 0, 1, 1)]
    second = [data[i : i + 1, :] for i in (1, 3, 2, 3, 2, 3)]
    holder = data[4:5, :]
    owner = [f // ROWS_LOC * N_COL + s // COLS_LOC for f, s in zip(first, second)]
    asked = jnp.zeros((1, 1024), jnp.int32)
    for o, f, s in zip(owner, first, second):
        asked += jnp.where((o == me) & (holder >= 0), f % ROWS_LOC * COLS_LOC + s % COLS_LOC + 1, 0)
    dev = lax.broadcasted_iota(jnp.int32, (DEVS, 1024), 0)
    hot = jnp.where(dev == holder, 1.0, 0.0).astype(BF16)
    wanted = jnp.broadcast_to(asked.astype(F32), (8, 1024)).astype(BF16)
    lid = lax.dot_general(wanted, hot, (((1,), (1,)), ((), ())), preferred_element_type=F32)[0:1].astype(jnp.int32)
    own = jnp.broadcast_to(jnp.where(holder == me, 1, 0), (8, 1024))
    lane = lax.broadcasted_iota(jnp.int32, (8, 1024), 1)
    count = own
    for shift in (1, 2, 4, 8, 16, 32, 64, 128, 256, 512):
        count = count + jnp.where(lane >= shift, pltpu.roll(count, shift, 1), 0)
    slot = lax.broadcasted_iota(jnp.int32, (8, 1024), 0)
    sel = (own > 0) & (count - 1 == slot)
    deg = jnp.sum(jnp.where(sel, data[5:6, :].astype(F32), 0.0), 1, keepdims=True)
    col = lax.broadcasted_iota(jnp.int32, (8, DEVS), 1)
    row = lax.broadcasted_iota(jnp.int32, (8, DEVS), 0)
    owners = jnp.zeros((8, DEVS), F32)
    back = jnp.zeros((8, DEVS), F32)
    for t in range(6):
        of = jnp.sum(jnp.where(sel, owner[t].astype(F32), 0.0), 1, keepdims=True)
        owners = jnp.where(col == t, of, owners)
        back += jnp.where((of == col.astype(F32)) & (deg > 0.0), (row * 6 + t).astype(F32), 0.0)
    back = jnp.sum(back, 0, keepdims=True).astype(jnp.int32)
    tabs[3:8, :] = jnp.zeros((5, DEVS), jnp.int32)
    lid = jnp.clip(lid, 0, BLOCKS)
    tabs[0:1, :] = jnp.maximum(lid - 1, 0)
    tabs[1:2, :] = jnp.where(lid > 0, lid - 1, BLOCKS)
    tabs[2:3, :] = jnp.clip(back, 0, 6 * SLOTS - 1)
    tabs[8:16, :] = jnp.clip(owners.astype(jnp.int32), 0, DEVS - 1)
    facs[...] = jnp.broadcast_to(deg, (8, DEVS))


def fused_kernel(
    quart, hold, degen, dens_hbm, integ, out, tabs_out,
    data, tabs_v, facs_v, tabs, facs, tab_sem,
    dens, a_all, g_all, work, send, recv0, recv1, give, d_nat, d_in, left, acc, o_acc, o_perm, perm, contrib,
    dens_sem, a_sem, send_sem, recv_sem, give_sem, back_sem, col_sem,
):
    recv = (recv0, recv1)
    dens_in = [pltpu.make_async_copy(dens_hbm.at[pl.ds(i * 4, 4)], dens.at[pl.ds(i * 4, 4)], dens_sem.at[i]) for i in range(4)]
    for copy in dens_in:
        copy.start()

    def load(q):
        return pltpu.make_async_copy(integ.at[q], a_all.at[q], a_sem.at[q])

    greet()
    count = hold.shape[1]
    data[...] = jnp.full(data.shape, -1, jnp.int32)
    data[0:4, :count] = quart[...]
    data[4:5, :count] = hold[...]
    data[5:6, :count] = degen[...]
    make_tables(data, tabs_v, facs_v)
    tab_in = [pltpu.make_async_copy(tabs_v, tabs, tab_sem.at[0]), pltpu.make_async_copy(facs_v, facs, tab_sem.at[1])]
    for copy in tab_in:
        copy.start()
    flat = work.reshape(160 * 64, 128)
    for i in range(4):
        dens_in[i].wait()

        def split(a, _):
            for ck in range(64):
                k, cc = ck // 8, ck % 8
                flat[pl.ds(a * 8 * PITCH + cc * 8 + k, 8, stride=PITCH), :] = dens[a, :, ck * 128 : (ck + 1) * 128]
            return 0

        lax.fori_loop(i * 4, i * 4 + 4, split, 0)
    greeted(col_sem)
    for q in range(SLOTS):
        load(q).start()
    blocks = work.at[pl.ds(0, 144)].reshape(BLOCKS, PITCH, 128)

    for copy in tab_in:
        copy.wait()
    tabs_out[...] = tabs_v[...]

    def choose(h, _):
        block = blocks[tabs[0, h]].astype(BF16)
        send[0, h] = block[:32]
        send[1, h] = block[32:64]
        return 0

    lax.fori_loop(0, DEVS, choose, 0)
    all_in(col_sem)
    for kh in range(2):
        post_all(send.at[kh], recv[kh], send_sem.at[kh], recv_sem.at[kh])
    perm[...] = half_perm()
    wide = work.reshape(8, 32 * GPITCH, 128)

    def regroup(q, _):
        load(q).wait()

        def widen(x, _):
            for uh in range(8):
                wide[uh, pl.ds(x * GPITCH, 32), :] = a_all[q, pl.ds(x * 32, 32), uh * 128 : (uh + 1) * 128].astype(F32)
            return 0

        lax.fori_loop(0, 32, widen, 0)

        def gather(y, _):
            for uh in range(8):
                g_all[q, pl.ds(y * 32, 32), uh * 128 : (uh + 1) * 128] = wide[uh, pl.ds(y, 32, stride=GPITCH), :].astype(BF16)
            return 0

        lax.fori_loop(0, 32, gather, 0)
        return 0

    lax.fori_loop(0, SLOTS, regroup, 0)
    def take_half(kh):
        all_of(send.at[kh], recv[kh], send_sem.at[kh], recv_sem.at[kh]).wait_recv()

        def collect(q, _):
            for t in range(6):
                d_nat[kh, q * 6 + t] = lanes_of(recv[kh][tabs[8 + q, t]].astype(F32))
            for n, t in enumerate((4, 2)):
                d_in[pl.ds(pl.multiple_of((q * 2 + n) * 8, 8), 8), :] = d_nat[kh, q * 6 + t]
            return 0

        lax.fori_loop(0, SLOTS, collect, 0)
        moved = jnp.dot(d_in[...].astype(BF16), perm[...], preferred_element_type=F32)
        for i in range(16):
            rows = moved[i * 8 : (i + 1) * 8]
            left[kh, i] = jnp.concatenate([rows[:, u * 128 : (u + 1) * 128] for u in range(4)], 0).astype(BF16)

    def coulomb(kh, q, qt):
        span = pl.ds(pl.multiple_of(qt * 256, 256), 256)
        base = q * 6
        j_pq = lax.dot_general(
            d_nat[kh, base + 1].astype(BF16),
            a_all[q, span, kh * 512 : (kh + 1) * 512],
            (((1,), (1,)), ((), ())),
            preferred_element_type=F32,
        )
        j_rs = jnp.dot(
            d_nat[kh, base].astype(BF16), a_all[q, kh * 512 : (kh + 1) * 512, span], preferred_element_type=F32
        )
        return two_rows(j_pq), two_rows(j_rs)

    def first_part(q, _):
        base = q * 6
        for qt in range(4):
            acc[qt, base], acc[qt, base + 1] = coulomb(0, q, qt)
            acc[qt, base + 3] = fold_quarter(a_all, q, left[0, q * 2], qt, 0)
            acc[qt, base + 5] = fold_quarter(g_all, q, left[0, q * 2 + 1], qt, 0)
        for hf in range(2):
            o_acc[hf, q * 2] = spread_half(a_all, q, d_nat[0, base + 3], hf, 0)
            o_acc[hf, q * 2 + 1] = spread_half(g_all, q, d_nat[0, base + 5], hf, 0)
        return 0

    take_half(0)
    lax.fori_loop(0, SLOTS, first_part, 0)
    take_half(1)

    def quarter(qt, hf, first):
        def one(q, _):
            base = q * 6
            coul = 2.0 * facs[q, 0]
            exch = -0.5 * facs[q, 0]
            j_pq, j_rs = coulomb(1, q, qt)
            contrib[qt, base] = (coul * (acc[qt, base] + j_pq)).astype(BF16)
            contrib[qt, base + 1] = (coul * (acc[qt, base + 1] + j_rs)).astype(BF16)
            k_ps = acc[qt, base + 3] + fold_quarter(a_all, q, left[1, q * 2], qt, 1)
            contrib[qt, base + 3] = (exch * k_ps).astype(BF16)
            k_qs = acc[qt, base + 5] + fold_quarter(g_all, q, left[1, q * 2 + 1], qt, 1)
            contrib[qt, base + 5] = (exch * k_qs).astype(BF16)
            if first:
                k_qr = o_acc[hf, q * 2] + spread_half(a_all, q, d_nat[1, base + 3], hf, 1)
                o_perm[q * 2] = exch * k_qr
                k_pr = o_acc[hf, q * 2 + 1] + spread_half(g_all, q, d_nat[1, base + 5], hf, 1)
                o_perm[q * 2 + 1] = exch * k_pr
            return 0

        lax.fori_loop(0, SLOTS, one, 0)
        if first:
            natural = lax.dot_general(
                o_perm[...].reshape(128, 512).astype(BF16), perm[...], (((1,), (1,)), ((), ())), preferred_element_type=F32
            )
            for i in range(16):
                at = (i // 2) * 6 + (4, 2)[i % 2]
                rows = natural[i * 8 : (i + 1) * 8]
                contrib[qt, at] = two_rows(rows[:, :256]).astype(BF16)
                contrib[qt + 1, at] = two_rows(rows[:, 256:]).astype(BF16)

        def place(i, _):
            for j in range(8):
                give[qt, i * 8 + j] = contrib[qt, tabs[2, i * 8 + j]]
            return 0

        lax.fori_loop(0, DEVS // 8, place, 0)
        post_all(give.at[qt], out.at[qt], give_sem.at[qt], back_sem.at[qt])

    def half(hf, _):
        quarter(hf * 2, hf, True)
        quarter(hf * 2 + 1, hf, False)
        return 0

    lax.fori_loop(0, 2, half, 0)
    for kh in range(2):
        all_of(send.at[kh], recv[kh], send_sem.at[kh], recv_sem.at[kh]).wait_send()
    for qt in range(4):
        done = all_of(give.at[qt], out.at[qt], give_sem.at[qt], back_sem.at[qt])
        done.wait_recv()
        done.wait_send()


def scatter_kernel(tabs, arrived, out, land, acc, whole, in_sem, out_sem):
    loads = [pltpu.make_async_copy(arrived.at[qt], land.at[qt], in_sem.at[qt]) for qt in range(4)]
    stores = [pltpu.make_async_copy(whole.at[pl.ds(i * 4, 4)], out.at[pl.ds(i * 4, 4)], out_sem.at[i]) for i in range(4)]
    for copy in loads:
        copy.start()

    def clear(i, _):
        acc[pl.ds(i * PITCH, PITCH), :] = jnp.zeros((PITCH, 128), F32)
        return 0

    lax.fori_loop(0, BLOCKS, clear, 0, unroll=4)
    for copy in loads:
        copy.wait()

    def add(h, _):
        at = pl.multiple_of(tabs[1, h] * PITCH, 8)
        more = jnp.concatenate([land[qt, h].astype(F32) for qt in range(4)], 0)
        acc[pl.ds(at, 64), :] += more
        return 0

    lax.fori_loop(0, DEVS, add, 0, unroll=4)
    for i in range(4):

        def join(a, _):
            for ck in range(64):
                k, c = ck // 8, ck % 8
                whole[a, :, ck * 128 : (ck + 1) * 128] = acc[pl.ds(a * 8 * PITCH + c * 8 + k, 8, stride=PITCH), :]
            return 0

        lax.fori_loop(i * 4, i * 4 + 4, join, 0)
        stores[i].start()
    for copy in stores:
        copy.wait()


def vspec():
    return pl.BlockSpec(memory_space=VMEM)


def sspec():
    return pl.BlockSpec(memory_space=SMEM)


def params(**kw):
    return pltpu.CompilerParams(vmem_limit_bytes=60 * 2**20, **kw)


def local(density, integrals, quartets, holder, degeneracy):
    anyspec = pl.BlockSpec(memory_space=pl.ANY)
    dma = pltpu.SemaphoreType.DMA
    arrived, tabs = pl.pallas_call(
        fused_kernel,
        out_shape=[jax.ShapeDtypeStruct((4, DEVS, 16, 128), BF16), jax.ShapeDtypeStruct((16, DEVS), jnp.int32)],
        in_specs=[vspec(), vspec(), vspec(), anyspec, anyspec],
        out_specs=[vspec(), vspec()],
        scratch_shapes=[
            VMEM((8, 1024), jnp.int32),
            VMEM((16, DEVS), jnp.int32),
            VMEM((8, DEVS), F32),
            SMEM((16, DEVS), jnp.int32),
            SMEM((8, DEVS), F32),
            dma((2,)),
            VMEM((ROWS_LOC, COLS_LOC, 8192), F32),
            VMEM((SLOTS, 1024, 1024), BF16),
            VMEM((SLOTS, 1024, 1024), BF16),
            VMEM((160, 64, 128), F32),
            VMEM((2, DEVS, 32, 128), BF16),
            VMEM((DEVS, 32, 128), BF16),
            VMEM((DEVS, 32, 128), BF16),
            VMEM((4, DEVS, 16, 128), BF16),
            VMEM((2, 48, 8, 512), F32),
            VMEM((128, 512), F32),
            VMEM((2, 16, 32, 128), BF16),
            VMEM((4, 48, 16, 128), F32),
            VMEM((2, 16, 8, 512), F32),
            VMEM((16, 8, 512), F32),
            VMEM((512, 512), BF16),
            VMEM((4, 48, 16, 128), BF16),
            dma((4,)),
            dma((SLOTS,)),
            dma((2,)),
            dma((2,)),
            dma((4,)),
            dma((4,)),
            pltpu.SemaphoreType.REGULAR,
        ],
        compiler_params=params(collective_id=0, has_side_effects=True),
        name="fused",
    )(quartets.T, holder[None], degeneracy[None], density, integrals)
    return pl.pallas_call(
        scatter_kernel,
        out_shape=jax.ShapeDtypeStruct(density.shape, F32),
        in_specs=[sspec(), anyspec],
        out_specs=anyspec,
        scratch_shapes=[
            VMEM((4, DEVS, 16, 128), BF16),
            VMEM(((BLOCKS + 1) * PITCH, 128), F32),
            VMEM(density.shape, F32),
            dma((4,)),
            dma((4,)),
        ],
        compiler_params=params(),
        name="scatter",
    )(tabs, arrived)


def solution(mesh):
    return jax.shard_map(
        local,
        mesh=mesh,
        in_specs=(P("row", "col", None), P(("row", "col"), None, None), P(), P(), P()),
        out_specs=P("row", "col", None),
        check_vma=False,
    )
```

```python
import jax
import jax.numpy as jnp
from jax import lax
from jax.experimental import pallas as pl
from jax.experimental.pallas import tpu as pltpu
from jax.sharding import PartitionSpec as P

BS = 32
PERT = 8
SLOTS = 8
N_ROW = 8
N_COL = 16
DEVS = N_ROW * N_COL
ROWS_LOC = 16
COLS_LOC = 8
BLOCKS = ROWS_LOC * COLS_LOC
PITCH = 72
GPITCH = 40
MESH = pl.DeviceIdType.MESH
F32 = jnp.float32
BF16 = jnp.bfloat16
VMEM = pltpu.VMEM
SMEM = pltpu.SMEM


def here():
    return lax.axis_index("row"), lax.axis_index("col")


def greet():
    r, c = here()
    first = pltpu.get_barrier_semaphore()

    def greet_row(i, _):
        pl.semaphore_signal(first, inc=1, device_id=((r + i) % N_ROW, c), device_id_type=MESH)
        return 0

    def greet_col(i, _):
        pl.semaphore_signal(first, inc=1, device_id=(r, (c + i) % N_COL), device_id_type=MESH)
        return 0

    lax.fori_loop(1, N_ROW, greet_row, 0)
    lax.fori_loop(1, N_COL, greet_col, 0)


def greeted(col_sem):
    r, c = here()

    def pass_on(i, _):
        pl.semaphore_signal(col_sem, inc=1, device_id=(r, (c + i) % N_COL), device_id_type=MESH)
        return 0

    pl.semaphore_wait(pltpu.get_barrier_semaphore(), N_ROW + N_COL - 2)
    lax.fori_loop(1, N_COL, pass_on, 0)


def all_in(col_sem):
    pl.semaphore_wait(col_sem, N_COL - 1)


def all_of(src, dst, send_sem, recv_sem):
    return pltpu.make_async_remote_copy(
        src_ref=src.at[pl.ds(0, DEVS - 1)],
        dst_ref=dst.at[pl.ds(0, DEVS - 1)],
        send_sem=send_sem,
        recv_sem=recv_sem,
        device_id=here(),
        device_id_type=MESH,
    )


def post(src, dst, send_sem, recv_sem, tr, tc):
    r, c = here()
    pltpu.make_async_remote_copy(
        src_ref=src.at[tr * N_COL + tc],
        dst_ref=dst.at[r * N_COL + c],
        send_sem=send_sem,
        recv_sem=recv_sem,
        device_id=(tr, tc),
        device_id_type=MESH,
    ).start()


def post_row(src, dst, send_sem, recv_sem, i):
    r, c = here()
    tr = lax.rem(r + i, N_ROW)
    for j in range(1, N_COL):
        post(src, dst, send_sem, recv_sem, tr, lax.rem(c + j, N_COL))

    @pl.when(i < N_ROW - 1)
    def _():
        post(src, dst, send_sem, recv_sem, lax.rem(r + i + 1, N_ROW), c)


def post_all(src, dst, send_sem, recv_sem):
    r, c = here()
    me = r * N_COL + c

    def row(i, _):
        post_row(src, dst, send_sem, recv_sem, i)
        return 0

    lax.fori_loop(0, N_ROW, row, 0)
    dst[me] = src[me]


def group_of(shape):
    return lax.broadcasted_iota(jnp.int32, shape, 1) // 32


def nat_fold(parts):
    g = group_of((8, 128))
    lo = g < 2
    ev = g % 2 == 0
    s = []
    for o in parts:
        s.append(jnp.where(g == 0, o[0:8], jnp.where(g == 1, o[8:16], jnp.where(g == 2, o[16:24], o[24:32]))))
    c02 = jnp.where(lo, s[0], s[2]) + pltpu.roll(jnp.where(lo, s[2], s[0]), 64, 1)
    c13 = jnp.where(lo, s[1], s[3]) + pltpu.roll(jnp.where(lo, s[3], s[1]), 64, 1)
    return jnp.where(ev, c02, c13) + jnp.where(ev, pltpu.roll(c02, 96, 1), pltpu.roll(c13, 32, 1))


def spread(d):
    g = group_of((8, 128))
    rolled = [d] + [pltpu.roll(d, 32 * i, 1) for i in range(1, 4)]
    return [
        jnp.concatenate([jnp.where(g == ul, rolled[(ul - xl) % 4], 0.0) for ul in range(4)], 0) for xl in range(4)
    ]


def half_tile(src, q, lead, hf):
    return jnp.concatenate(
        [src[q, pl.ds(pl.multiple_of(lead * 32 + hf * 16, 16), 16), uh * 128 : (uh + 1) * 128] for uh in range(8)], 0
    )


def fold_quarter(src, q, left, qt, kh):
    outs = []
    for grp in range(2):
        parts = []
        for pair in range(2):
            lead = qt * 8 + grp * 4 + pair * 2
            w = jnp.concatenate([half_tile(src, q, lead, kh), half_tile(src, q, lead + 1, kh)], 1)
            o = jnp.dot(left, w, preferred_element_type=F32)
            parts += [o[:, :128], o[:, 128:]]
        outs.append(nat_fold(parts))
    return jnp.concatenate(outs, 0)


def spread_half(src, q, d, hf, kh):
    acc = jnp.zeros((32, 128), F32)
    for grp in range(4):
        exp = spread(d[:, grp * 128 : (grp + 1) * 128])
        for pair in range(2):
            lead = kh * 16 + grp * 4 + pair * 2
            w = jnp.concatenate([half_tile(src, q, lead, hf), half_tile(src, q, lead + 1, hf)], 1)
            e = jnp.concatenate([exp[pair * 2], exp[pair * 2 + 1]], 1).astype(BF16)
            acc = acc + lax.dot_general(e, w, (((1,), (1,)), ((), ())), preferred_element_type=F32)
    return jnp.concatenate([acc[u * 8 : (u + 1) * 8] for u in range(4)], 1)


def half_perm():
    i = lax.broadcasted_iota(jnp.int32, (512, 512), 0)
    j = lax.broadcasted_iota(jnp.int32, (512, 512), 1)
    return jnp.where((i % 4) * 128 + ((i // 4) % 8) * 16 + i // 32 == j, 1.0, 0.0).astype(BF16)


def two_rows(x):
    return jnp.concatenate([x[:, :128], x[:, 128:]], 0)


def lanes_of(x):
    return jnp.concatenate([x[c * 8 : (c + 1) * 8, :] for c in range(x.shape[0] // 8)], 1)


def make_tables(data, tabs, facs):
    r, c = here()
    me = r * N_COL + c
    first = [data[i : i + 1, :] for i in (0, 2, 0, 0, 1, 1)]
    second = [data[i : i + 1, :] for i in (1, 3, 2, 3, 2, 3)]
    holder = data[4:5, :]
    owner = [f // ROWS_LOC * N_COL + s // COLS_LOC for f, s in zip(first, second)]
    asked = jnp.zeros((1, 1024), jnp.int32)
    for o, f, s in zip(owner, first, second):
        asked += jnp.where((o == me) & (holder >= 0), f % ROWS_LOC * COLS_LOC + s % COLS_LOC + 1, 0)
    dev = lax.broadcasted_iota(jnp.int32, (DEVS, 1024), 0)
    hot = jnp.where(dev == holder, 1.0, 0.0).astype(BF16)
    wanted = jnp.broadcast_to(asked.astype(F32), (8, 1024)).astype(BF16)
    lid = lax.dot_general(wanted, hot, (((1,), (1,)), ((), ())), preferred_element_type=F32)[0:1].astype(jnp.int32)
    own = jnp.broadcast_to(jnp.where(holder == me, 1, 0), (8, 1024))
    lane = lax.broadcasted_iota(jnp.int32, (8, 1024), 1)
    count = own
    for shift in (1, 2, 4, 8, 16, 32, 64, 128, 256, 512):
        count = count + jnp.where(lane >= shift, pltpu.roll(count, shift, 1), 0)
    slot = lax.broadcasted_iota(jnp.int32, (8, 1024), 0)
    sel = (own > 0) & (count - 1 == slot)
    deg = jnp.sum(jnp.where(sel, data[5:6, :].astype(F32), 0.0), 1, keepdims=True)
    col = lax.broadcasted_iota(jnp.int32, (8, DEVS), 1)
    row = lax.broadcasted_iota(jnp.int32, (8, DEVS), 0)
    owners = jnp.zeros((8, DEVS), F32)
    back = jnp.zeros((8, DEVS), F32)
    for t in range(6):
        of = jnp.sum(jnp.where(sel, owner[t].astype(F32), 0.0), 1, keepdims=True)
        owners = jnp.where(col == t, of, owners)
        back += jnp.where((of == col.astype(F32)) & (deg > 0.0), (row * 6 + t).astype(F32), 0.0)
    back = jnp.sum(back, 0, keepdims=True).astype(jnp.int32)
    tabs[3:8, :] = jnp.zeros((5, DEVS), jnp.int32)
    lid = jnp.clip(lid, 0, BLOCKS)
    tabs[0:1, :] = jnp.maximum(lid - 1, 0)
    tabs[1:2, :] = jnp.where(lid > 0, lid - 1, BLOCKS)
    tabs[2:3, :] = jnp.clip(back, 0, 6 * SLOTS - 1)
    tabs[8:16, :] = jnp.clip(owners.astype(jnp.int32), 0, DEVS - 1)
    facs[...] = jnp.broadcast_to(deg, (8, DEVS))


def fused_kernel(
    quart, hold, degen, dens_hbm, integ, out, tabs_out,
    data, tabs_v, facs_v, tabs, facs, tab_sem,
    dens, a_all, g_all, work, send, recv0, recv1, give, d_nat, d_in, left, acc, o_acc, o_perm, perm, contrib,
    dens_sem, a_sem, send_sem, recv_sem, give_sem, back_sem, col_sem,
):
    recv = (recv0, recv1)
    dens_in = [pltpu.make_async_copy(dens_hbm.at[pl.ds(i * 4, 4)], dens.at[pl.ds(i * 4, 4)], dens_sem.at[i]) for i in range(4)]
    for copy in dens_in:
        copy.start()

    def load(q):
        return pltpu.make_async_copy(integ.at[q], a_all.at[q], a_sem.at[q])

    greet()
    count = hold.shape[1]
    data[...] = jnp.full(data.shape, -1, jnp.int32)
    data[0:4, :count] = quart[...]
    data[4:5, :count] = hold[...]
    data[5:6, :count] = degen[...]
    make_tables(data, tabs_v, facs_v)
    tab_in = [pltpu.make_async_copy(tabs_v, tabs, tab_sem.at[0]), pltpu.make_async_copy(facs_v, facs, tab_sem.at[1])]
    for copy in tab_in:
        copy.start()
    flat = work.reshape(160 * 64, 128)
    for i in range(4):
        dens_in[i].wait()

        def split(a, _):
            for ck in range(64):
                k, cc = ck // 8, ck % 8
                flat[pl.ds(a * 8 * PITCH + cc * 8 + k, 8, stride=PITCH), :] = dens[a, :, ck * 128 : (ck + 1) * 128]
            return 0

        lax.fori_loop(i * 4, i * 4 + 4, split, 0)
    greeted(col_sem)
    for q in range(SLOTS):
        load(q).start()
    blocks = work.at[pl.ds(0, 144)].reshape(BLOCKS, PITCH, 128)

    for copy in tab_in:
        copy.wait()
    tabs_out[...] = tabs_v[...]

    def choose(h, _):
        block = blocks[tabs[0, h]].astype(BF16)
        send[0, h] = block[:32]
        send[1, h] = block[32:64]
        return 0

    lax.fori_loop(0, DEVS, choose, 0)
    all_in(col_sem)
    for kh in range(2):
        post_all(send.at[kh], recv[kh], send_sem.at[kh], recv_sem.at[kh])
    perm[...] = half_perm()
    wide = work.reshape(8, 32 * GPITCH, 128)

    def regroup(q, _):
        load(q).wait()

        def widen(x, _):
            for uh in range(8):
                wide[uh, pl.ds(x * GPITCH, 32), :] = a_all[q, pl.ds(x * 32, 32), uh * 128 : (uh + 1) * 128].astype(F32)
            return 0

        lax.fori_loop(0, 32, widen, 0)

        def gather(y, _):
            for uh in range(8):
                g_all[q, pl.ds(y * 32, 32), uh * 128 : (uh + 1) * 128] = wide[uh, pl.ds(y, 32, stride=GPITCH), :].astype(BF16)
            return 0

        lax.fori_loop(0, 32, gather, 0)
        return 0

    lax.fori_loop(0, SLOTS, regroup, 0)
    def take_half(kh):
        all_of(send.at[kh], recv[kh], send_sem.at[kh], recv_sem.at[kh]).wait_recv()

        def collect(q, _):
            for t in range(6):
                d_nat[kh, q * 6 + t] = lanes_of(recv[kh][tabs[8 + q, t]].astype(F32))
            for n, t in enumerate((4, 2)):
                d_in[pl.ds(pl.multiple_of((q * 2 + n) * 8, 8), 8), :] = d_nat[kh, q * 6 + t]
            return 0

        lax.fori_loop(0, SLOTS, collect, 0)
        moved = jnp.dot(d_in[...].astype(BF16), perm[...], preferred_element_type=F32)
        for i in range(16):
            rows = moved[i * 8 : (i + 1) * 8]
            left[kh, i] = jnp.concatenate([rows[:, u * 128 : (u + 1) * 128] for u in range(4)], 0).astype(BF16)

    def coulomb(kh, q, qt):
        span = pl.ds(pl.multiple_of(qt * 256, 256), 256)
        base = q * 6
        j_pq = lax.dot_general(
            d_nat[kh, base + 1].astype(BF16),
            a_all[q, span, kh * 512 : (kh + 1) * 512],
            (((1,), (1,)), ((), ())),
            preferred_element_type=F32,
        )
        j_rs = jnp.dot(
            d_nat[kh, base].astype(BF16), a_all[q, kh * 512 : (kh + 1) * 512, span], preferred_element_type=F32
        )
        return two_rows(j_pq), two_rows(j_rs)

    def first_part(q, _):
        base = q * 6
        for qt in range(4):
            acc[qt, base], acc[qt, base + 1] = coulomb(0, q, qt)
            acc[qt, base + 3] = fold_quarter(a_all, q, left[0, q * 2], qt, 0)
            acc[qt, base + 5] = fold_quarter(g_all, q, left[0, q * 2 + 1], qt, 0)
        for hf in range(2):
            o_acc[hf, q * 2] = spread_half(a_all, q, d_nat[0, base + 3], hf, 0)
            o_acc[hf, q * 2 + 1] = spread_half(g_all, q, d_nat[0, base + 5], hf, 0)
        return 0

    take_half(0)
    lax.fori_loop(0, SLOTS, first_part, 0)
    take_half(1)

    def quarter(qt, hf, first):
        def one(q, _):
            base = q * 6
            coul = 2.0 * facs[q, 0]
            exch = -0.5 * facs[q, 0]
            j_pq, j_rs = coulomb(1, q, qt)
            contrib[qt, base] = (coul * (acc[qt, base] + j_pq)).astype(BF16)
            contrib[qt, base + 1] = (coul * (acc[qt, base + 1] + j_rs)).astype(BF16)
            k_ps = acc[qt, base + 3] + fold_quarter(a_all, q, left[1, q * 2], qt, 1)
            contrib[qt, base + 3] = (exch * k_ps).astype(BF16)
            k_qs = acc[qt, base + 5] + fold_quarter(g_all, q, left[1, q * 2 + 1], qt, 1)
            contrib[qt, base + 5] = (exch * k_qs).astype(BF16)
            if first:
                k_qr = o_acc[hf, q * 2] + spread_half(a_all, q, d_nat[1, base + 3], hf, 1)
                o_perm[q * 2] = exch * k_qr
                k_pr = o_acc[hf, q * 2 + 1] + spread_half(g_all, q, d_nat[1, base + 5], hf, 1)
                o_perm[q * 2 + 1] = exch * k_pr
            return 0

        lax.fori_loop(0, SLOTS, one, 0)
        if first:
            natural = lax.dot_general(
                o_perm[...].reshape(128, 512).astype(BF16), perm[...], (((1,), (1,)), ((), ())), preferred_element_type=F32
            )
            for i in range(16):
                at = (i // 2) * 6 + (4, 2)[i % 2]
                rows = natural[i * 8 : (i + 1) * 8]
                contrib[qt, at] = two_rows(rows[:, :256]).astype(BF16)
                contrib[qt + 1, at] = two_rows(rows[:, 256:]).astype(BF16)

        def place(i, _):
            r, c = here()
            tr = lax.rem(r + i, N_ROW)
            ends = give.at[qt], out.at[qt], give_sem.at[qt], back_sem.at[qt]
            for j in range(N_COL):
                give[qt, tr * N_COL + j] = contrib[qt, tabs[2, tr * N_COL + j]]
            for j in range(1, N_COL):
                post(*ends, tr, lax.rem(c + j, N_COL))

            @pl.when(i > 0)
            def _():
                post(*ends, tr, c)

            return 0

        lax.fori_loop(0, N_ROW, place, 0)
        r, c = here()
        out[qt, r * N_COL + c] = give[qt, r * N_COL + c]

    def half(hf, _):
        quarter(hf * 2, hf, True)
        quarter(hf * 2 + 1, hf, False)
        return 0

    lax.fori_loop(0, 2, half, 0)
    for kh in range(2):
        all_of(send.at[kh], recv[kh], send_sem.at[kh], recv_sem.at[kh]).wait_send()
    for qt in range(4):
        done = all_of(give.at[qt], out.at[qt], give_sem.at[qt], back_sem.at[qt])
        done.wait_recv()
        done.wait_send()


def scatter_kernel(tabs, arrived, out, land, acc, whole, in_sem, out_sem):
    loads = [pltpu.make_async_copy(arrived.at[qt], land.at[qt], in_sem.at[qt]) for qt in range(4)]
    stores = [pltpu.make_async_copy(whole.at[pl.ds(i * 4, 4)], out.at[pl.ds(i * 4, 4)], out_sem.at[i]) for i in range(4)]
    for copy in loads:
        copy.start()

    def clear(i, _):
        acc[pl.ds(i * PITCH, PITCH), :] = jnp.zeros((PITCH, 128), F32)
        return 0

    lax.fori_loop(0, BLOCKS, clear, 0, unroll=4)
    for copy in loads:
        copy.wait()

    def add(h, _):
        at = pl.multiple_of(tabs[1, h] * PITCH, 8)
        more = jnp.concatenate([land[qt, h].astype(F32) for qt in range(4)], 0)
        acc[pl.ds(at, 64), :] += more
        return 0

    lax.fori_loop(0, DEVS, add, 0, unroll=4)
    for i in range(4):

        def join(a, _):
            for ck in range(64):
                k, c = ck // 8, ck % 8
                whole[a, :, ck * 128 : (ck + 1) * 128] = acc[pl.ds(a * 8 * PITCH + c * 8 + k, 8, stride=PITCH), :]
            return 0

        lax.fori_loop(i * 4, i * 4 + 4, join, 0)
        stores[i].start()
    for copy in stores:
        copy.wait()


def vspec():
    return pl.BlockSpec(memory_space=VMEM)


def sspec():
    return pl.BlockSpec(memory_space=SMEM)


def params(**kw):
    return pltpu.CompilerParams(vmem_limit_bytes=60 * 2**20, **kw)


def local(density, integrals, quartets, holder, degeneracy):
    anyspec = pl.BlockSpec(memory_space=pl.ANY)
    dma = pltpu.SemaphoreType.DMA
    arrived, tabs = pl.pallas_call(
        fused_kernel,
        out_shape=[jax.ShapeDtypeStruct((4, DEVS, 16, 128), BF16), jax.ShapeDtypeStruct((16, DEVS), jnp.int32)],
        in_specs=[vspec(), vspec(), vspec(), anyspec, anyspec],
        out_specs=[vspec(), vspec()],
        scratch_shapes=[
            VMEM((8, 1024), jnp.int32),
            VMEM((16, DEVS), jnp.int32),
            VMEM((8, DEVS), F32),
            SMEM((16, DEVS), jnp.int32),
            SMEM((8, DEVS), F32),
            dma((2,)),
            VMEM((ROWS_LOC, COLS_LOC, 8192), F32),
            VMEM((SLOTS, 1024, 1024), BF16),
            VMEM((SLOTS, 1024, 1024), BF16),
            VMEM((160, 64, 128), F32),
            VMEM((2, DEVS, 32, 128), BF16),
            VMEM((DEVS, 32, 128), BF16),
            VMEM((DEVS, 32, 128), BF16),
            VMEM((4, DEVS, 16, 128), BF16),
            VMEM((2, 48, 8, 512), F32),
            VMEM((128, 512), F32),
            VMEM((2, 16, 32, 128), BF16),
            VMEM((4, 48, 16, 128), F32),
            VMEM((2, 16, 8, 512), F32),
            VMEM((16, 8, 512), F32),
            VMEM((512, 512), BF16),
            VMEM((4, 48, 16, 128), BF16),
            dma((4,)),
            dma((SLOTS,)),
            dma((2,)),
            dma((2,)),
            dma((4,)),
            dma((4,)),
            pltpu.SemaphoreType.REGULAR,
        ],
        compiler_params=params(collective_id=0, has_side_effects=True),
        name="fused",
    )(quartets.T, holder[None], degeneracy[None], density, integrals)
    return pl.pallas_call(
        scatter_kernel,
        out_shape=jax.ShapeDtypeStruct(density.shape, F32),
        in_specs=[sspec(), anyspec],
        out_specs=anyspec,
        scratch_shapes=[
            VMEM((4, DEVS, 16, 128), BF16),
            VMEM(((BLOCKS + 1) * PITCH, 128), F32),
            VMEM(density.shape, F32),
            dma((4,)),
            dma((4,)),
        ],
        compiler_params=params(),
        name="scatter",
    )(tabs, arrived)


def solution(mesh):
    return jax.shard_map(
        local,
        mesh=mesh,
        in_specs=(P("row", "col", None), P(("row", "col"), None, None), P(), P(), P()),
        out_specs=P("row", "col", None),
        check_vma=False,
    )
```
